32 devices in a mesh: grp: 2 (over y), samp: 4 (over z), snp: 4 (over x, core).
Axes of the slice: x: 2, y: 2, z: 4, core: 2. Of those that a mesh axis runs over, the one named last changes fastest.
Arguments:
- genotypes: int32 [2048, 8192], P(('grp', 'samp'), 'snp'), parts along dimension 0, may hold values from 0 to 2730, as said below
- basis_cols: bfloat16 [16384, 256], P(('grp', 'snp')), parts along dimension 0, may hold values from -0.0625 to 0.0625
Outputs:
- y_block: float32 [8, 4, 512, 256], P(('grp', 'snp'), 'samp'), parts along dimension 0
- r_factor: float32 [512, 256], P('grp'), parts along dimension 0
- q_next: float32 [8, 4, 512, 256], P(('grp', 'snp'), 'samp'), parts along dimension 0
The draws below stay inside these ranges and needn't reach their ends.
There are 2 independent parts, one for each index of `grp`. The reference program is written for one: setup_inputs(seed, part) draws one part's arguments, and reference() takes and returns one part's arrays. A program takes and returns all parts, laid end to end along the dimension named above; each array names one. Nothing has to cross between parts.
Inputs may be any that keep to these rules, and one draw needn't show every extreme that they name: `genotypes`: each word packs 6 dosages of 0, 1 or 2 in pairs of bits: bits 2 t and 2 t + 1 of word (w, p) hold the dosage of sample 6 w + t at SNP p, t from 0 to 5; bits 12 and up are zero.
All inputs are finite; a program needn't handle non-finite values.
Results may differ from the reference program's by a relative error of at most 0.0025.
Values may be sent and summed in bfloat16 or wider, within the bound.
No kernel may reach another device: no remote copies, remote signals or barrier semaphores. Data moves between devices by JAX's collectives and lax.ppermute only.
A program may use at most 64 MiB of HBM per device.

```python
import math
import jax
import jax.numpy as jnp
from jax import lax

K = 256
PD = 2048
WD = 256
NP = 8192
N_SAMP = 4
N_SNP = 4


def draw_genotypes(key, part):
    key_base = jax.random.fold_in(key, 11)
    key_drift = jax.random.fold_in(key, 12)
    key_dose = jax.random.fold_in(key, 13)
    word_count = WD * N_SAMP
    snp_count = PD * N_SNP
    base_freq = jax.random.randint(key_base, (snp_count,), 10, 91)
    drift_level = jax.random.randint(key_drift, (N_SAMP, snp_count), 0, 3)
    frequency = base_freq[None, :] * (1 + drift_level) // 3
    freq_rows = jnp.repeat(frequency, WD, axis=0)
    packed = jnp.zeros((word_count, snp_count), jnp.int32)
    for plane_idx in range(6):
        plane_key = jax.random.fold_in(key_dose, plane_idx)
        first_draw = jax.random.randint(jax.random.fold_in(plane_key, 1), (word_count, snp_count), 0, 100)
        second_draw = jax.random.randint(jax.random.fold_in(plane_key, 2), (word_count, snp_count), 0, 100)
        dose_plane = (first_draw < freq_rows).astype(jnp.int32) + (second_draw < freq_rows).astype(jnp.int32)
        packed = packed + dose_plane * 4 ** plane_idx
    return packed


def levels(own_key, dims, pieces, least, top_value):
    level = 1.0
    for dim, parts in pieces:
        heights = jax.random.uniform(jax.random.fold_in(jax.random.fold_in(own_key, 6), dim), (parts,), jnp.float32, least / len(pieces), top_value / len(pieces))
        level = level * jnp.repeat(jnp.exp(heights), dims[dim] // parts).reshape((-1,) + (1,) * (len(dims) - 1 - dim))
    return level


def scatter_about(own_key, dims, deviation, reach, cuts=(), held_as=jnp.bfloat16):
    loudness = levels(own_key, dims, cuts, -0.22, 0.18) if cuts else 1.0
    drawn = jax.random.normal(own_key, dims, jnp.float32) * deviation * loudness
    return jnp.minimum(jnp.maximum(drawn, -reach), reach).astype(held_as)


def setup_inputs(seed: int = 0, part: int = 0) -> dict:
    arg_keys = jax.random.split(jax.random.key(seed), 3)
    part_keys = jax.random.split(jax.random.fold_in(arg_keys[2], part), 3)
    genotypes = draw_genotypes(jax.random.fold_in(jax.random.fold_in(arg_keys[2], part), 71), part)
    basis_cols = scatter_about(part_keys[1], (NP, K), NP ** -0.5, 0.0625, ((0, 4),))
    return {"genotypes": genotypes, "basis_cols": basis_cols}


def unpack(word_block):
    planes = [jnp.bitwise_and(jnp.right_shift(word_block, 2 * shift_pos), 3) for shift_pos in range(6)]
    return jnp.stack(planes, axis=1).reshape(word_block.shape[0] * 6, word_block.shape[1])

def reference(genotypes, basis_cols):
    word_count, snp_count = genotypes.shape
    samples = word_count * 6
    block_words = math.gcd(word_count, 64)
    blocks = genotypes.reshape(word_count // block_words, block_words, snp_count)

    def count_block(running, word_block):
        return (running + lax.optimization_barrier(jnp.sum(unpack(word_block), axis=0)).astype(jnp.int32), None)
    counts, unused = lax.scan(count_block, jnp.zeros((snp_count,), jnp.int32), blocks)
    allele_mean = counts.astype(jnp.float32) / jnp.float32(samples)
    center = jnp.dot(allele_mean, basis_cols.astype(jnp.float32), precision=lax.Precision.HIGHEST)

    def project_block(running, word_block):
        dosage = unpack(word_block).astype(jnp.bfloat16)
        scores = (jnp.dot(dosage.astype(jnp.float32), basis_cols.astype(jnp.float32), preferred_element_type=jnp.float32) - center[None, :]).astype(jnp.bfloat16)
        return (running + lax.dot_general(dosage.astype(jnp.float32), scores.astype(jnp.float32), (((0,), (0,)), ((), ())), preferred_element_type=jnp.float32), None)
    y_full, unused = lax.scan(project_block, jnp.zeros((snp_count, basis_cols.shape[1]), jnp.float32), blocks)
    y_full = y_full * (jnp.float32(1.0) / jnp.sqrt(jnp.float32(samples)))
    gram_sum = jnp.dot(y_full.T, y_full, precision=lax.Precision.HIGHEST) / jnp.float32(snp_count)
    lower_factor = jnp.linalg.cholesky(gram_sum)
    q_next = lax.linalg.triangular_solve(lower_factor, y_full, left_side=False, lower=True, transpose_a=True)
    layout = (N_SNP, N_SAMP, snp_count // (N_SNP * N_SAMP), basis_cols.shape[1])
    return (y_full.reshape(layout), lower_factor.T, q_next.reshape(layout))
```

```python
import functools

import jax
import jax.numpy as jnp
from jax import lax
from jax.experimental import pallas as pl
from jax.experimental.pallas import tpu as pltpu
from jax.sharding import PartitionSpec as P

PLANES = 6
STEPS = 64.0
TOP = 32767.0
HIGH = lax.Precision.HIGHEST
VMEM_BYTES = 40 * 1024 * 1024


def params(**more):
    return pltpu.CompilerParams(vmem_limit_bytes=VMEM_BYTES, **more)


def planes_of(words):
    return [
        jnp.bitwise_and(jnp.right_shift(words, 2 * t), 3).astype(jnp.float32).astype(jnp.bfloat16)
        for t in range(PLANES)
    ]


def project_kernel(pick, words, basis, out, sums):
    blocks, _, depth, _ = out.shape
    total = jnp.zeros(sums.shape, jnp.float32)
    for t, plane in enumerate(planes_of(words[...])):
        product = jnp.dot(plane, basis[...], preferred_element_type=jnp.float32)
        for b in range(blocks):
            out[b, t] = product[b * depth : (b + 1) * depth]
        total = total + product.reshape(-1, 8, product.shape[1]).sum(axis=0)
    sums[...] = total


def project(words, basis, pick, blocks):
    count, snps = words.shape
    width = basis.shape[1]
    half = count // 2
    depth = half // blocks
    return pl.pallas_call(
        project_kernel,
        grid_spec=pltpu.PrefetchScalarGridSpec(
            num_scalar_prefetch=1,
            grid=(1,),
            in_specs=[
                pl.BlockSpec((half, snps), lambda i, pick: (pick[0], 0)),
                pl.BlockSpec((snps, width), lambda i, pick: (0, 0)),
            ],
            out_specs=[
                pl.BlockSpec((blocks, PLANES, depth, width), lambda i, pick: (0, 0, 0, 0)),
                pl.BlockSpec((8, width), lambda i, pick: (0, 0)),
            ],
        ),
        out_shape=[
            jax.ShapeDtypeStruct((blocks, PLANES, depth, width), jnp.float32),
            jax.ShapeDtypeStruct((8, width), jnp.float32),
        ],
        compiler_params=params(),
        name="project",
        cost_estimate=pl.CostEstimate(
            flops=2 * half * PLANES * snps * width,
            bytes_accessed=4 * half * snps + 2 * snps * width + 4 * half * PLANES * width,
            transcendentals=0,
        ),
    )(pick, words, basis)


def bit_reverse(index, bits):
    out = 0
    for b in range(bits):
        out |= ((index >> b) & 1) << (bits - 1 - b)
    return out


def back_project(words, scores, scale):
    blocks = scores.shape[0]
    bits = blocks.bit_length() - 1
    total = None
    for t, plane in enumerate(planes_of(words)):
        rows = jnp.concatenate([scores[bit_reverse(b, bits), t] for b in range(blocks)], axis=0)
        term = lax.dot_general(
            rows, plane, (((0,), (0,)), ((), ())), preferred_element_type=jnp.float32
        )
        total = term if total is None else total + term
    return (total * scale).T


def sent_kernel(scale, pick, words, scores, out):
    value = back_project(words[...], scores, scale)
    rows = value.shape[0]
    top = jnp.maximum(jnp.max(jnp.abs(value), axis=0, keepdims=True), 1e-30)
    level = jnp.ceil(STEPS * jnp.log2(top / TOP)) + 1.0
    unit = jnp.exp2(level * (1.0 / STEPS))
    coded = jnp.clip(jnp.round(value * (1.0 / unit)), -TOP, TOP)
    out[:rows] = coded.astype(jnp.int32).astype(jnp.int16)
    out[rows:] = jnp.broadcast_to(level, (16, level.shape[1])).astype(jnp.int32).astype(jnp.int16)


def kept_kernel(scale, pick, words, scores, out):
    out[...] = back_project(words[...], scores, scale)


def chunk_of_y(words, scores, pick, rows, scale, sent):
    count, snps = words.shape
    width = scores.shape[-1]
    shape = (rows + 16, width) if sent else (rows, width)
    dtype = jnp.int16 if sent else jnp.float32
    return pl.pallas_call(
        functools.partial(sent_kernel if sent else kept_kernel, scale),
        grid_spec=pltpu.PrefetchScalarGridSpec(
            num_scalar_prefetch=1,
            grid=(1,),
            in_specs=[
                pl.BlockSpec((count, rows), lambda i, pick: (0, pick[0])),
                pl.BlockSpec(scores.shape, lambda i, pick: (0, 0, 0, 0)),
            ],
            out_specs=pl.BlockSpec(shape, lambda i, pick: (0, 0)),
        ),
        out_shape=jax.ShapeDtypeStruct(shape, dtype),
        compiler_params=params(),
        name="chunk_sent" if sent else "chunk_kept",
        cost_estimate=pl.CostEstimate(
            flops=2 * count * PLANES * rows * width,
            bytes_accessed=4 * count * rows + 2 * scores.size + 4 * rows * width,
            transcendentals=0,
        ),
    )(pick, words, scores)


def collect_kernel(scale, *refs):
    kept, out, gram = refs[0], refs[-2], refs[-1]
    rows = kept.shape[0]
    total = kept[...]
    for ref in refs[1:-2]:
        level = ref[rows : rows + 16].astype(jnp.int32).astype(jnp.float32)[:1]
        unit = jnp.exp2(level * (1.0 / STEPS))
        total = total + ref[:rows].astype(jnp.int32).astype(jnp.float32) * unit
    out[...] = total
    gram[...] = scale * lax.dot_general(
        total, total, (((0,), (0,)), ((), ())), precision=HIGH, preferred_element_type=jnp.float32
    )


def collect(kept, received, scale):
    width = kept.shape[1]
    return pl.pallas_call(
        functools.partial(collect_kernel, scale),
        out_shape=[
            jax.ShapeDtypeStruct(kept.shape, jnp.float32),
            jax.ShapeDtypeStruct((width, width), jnp.float32),
        ],
        compiler_params=params(),
        name="collect",
    )(kept, *received)


def swap(array, axis, mask):
    size = lax.axis_size(axis)
    return lax.ppermute(array, axis, [(i, i ^ mask) for i in range(size)])


def halve(array, axis, mask):
    bit = (lax.axis_index(axis) & mask) // mask
    mine = lax.dynamic_index_in_dim(array, bit, 0, keepdims=False)
    other = lax.dynamic_index_in_dim(array, 1 - bit, 0, keepdims=False)
    return mine, swap(other, axis, mask)


def gram_total(gram):
    width = gram.shape[0]
    n_snp, n_samp = lax.axis_size("snp"), lax.axis_size("samp")
    if n_snp != 4 or n_samp != 4:
        return lax.psum(gram, ("samp", "snp"))
    mine, got = halve(gram.reshape(2, width // 2, width), "snp", 1)
    part = mine + got
    mine, got = halve(part.reshape(2, width // 4, width), "snp", 2)
    part = mine + got
    part = ((part + swap(part, "samp", 1)) + (swap(part, "samp", 2) + swap(part, "samp", 3)))
    x_bit = (lax.axis_index("snp") // 2) == 0
    c_bit = (lax.axis_index("snp") % 2) == 0
    got = swap(part, "snp", 2)
    part = jnp.concatenate([jnp.where(x_bit, part, got), jnp.where(x_bit, got, part)], axis=0)
    got = swap(part, "snp", 1)
    return jnp.concatenate([jnp.where(c_bit, part, got), jnp.where(c_bit, got, part)], axis=0)


def per_device(genotypes, basis_cols):
    n_snp, n_samp = lax.axis_size("snp"), lax.axis_size("samp")
    bits = n_snp.bit_length() - 1
    words, snps = genotypes.shape
    width = basis_cols.shape[1]
    samples = words * PLANES * n_samp
    inv_root = float(1.0 / samples**0.5)
    blocks = n_snp // 2
    depth = words // n_snp
    me = lax.axis_index("snp")
    low = (me & 1).astype(jnp.int32)

    other, other_sums = project(genotypes, basis_cols, (1 - low)[None], blocks)
    got = swap(other, "snp", 1)
    mine, mine_sums = project(genotypes, basis_cols, low[None], blocks)
    part = mine + got
    sums = mine_sums + other_sums
    for b in range(1, bits):
        shape = (2, part.shape[0] // 2) + part.shape[1:]
        keep, got = halve(part.reshape(shape), "snp", 1 << b)
        part = keep + got
    if n_snp * n_samp <= 16:
        every = jnp.broadcast_to(sums[None], (n_snp * n_samp,) + sums.shape)
        center = lax.all_to_all(every, ("samp", "snp"), 0, 0, tiled=True).sum(axis=(0, 1))
    else:
        center = lax.psum(sums, ("samp", "snp")).sum(axis=0)
    center = center / jnp.float32(samples)
    rows = (part.reshape(PLANES * depth, width) - center[None, :]).astype(jnp.bfloat16)
    scores = lax.all_gather(rows, "snp").reshape(n_snp, PLANES, depth, width)

    chunk = snps // n_samp
    z = lax.axis_index("samp").astype(jnp.int32)
    total_snps = snps * n_snp
    if n_samp <= 4 and chunk % 128 == 0:
        received = []
        for mask in range(n_samp - 1, 0, -1):
            coded = chunk_of_y(genotypes, scores, (z ^ mask)[None], chunk, inv_root, True)
            received.append(swap(coded, "samp", mask))
        kept = chunk_of_y(genotypes, scores, z[None], chunk, inv_root, False)
        y_local, gram = collect(kept, received, 1.0 / total_snps)
    else:
        tile = 512 if snps % 512 == 0 else snps
        parts = [
            chunk_of_y(genotypes, scores, jnp.full((1,), i, jnp.int32), tile, inv_root, False)
            for i in range(snps // tile)
        ]
        y_local = lax.psum_scatter(
            jnp.concatenate(parts, axis=0), "samp", scatter_dimension=0, tiled=True
        )
        y_local, gram = collect(y_local, [], 1.0 / total_snps)
    gram_sum = gram_total(gram)
    lower_factor = jnp.linalg.cholesky(gram_sum)
    q_next = lax.linalg.triangular_solve(
        lower_factor, y_local, left_side=False, lower=True, transpose_a=True
    )
    layout = (1, 1, y_local.shape[0], width)
    return (y_local.reshape(layout), lower_factor.T, q_next.reshape(layout))


def solution(mesh):
    return jax.shard_map(
        per_device,
        mesh=mesh,
        in_specs=(P(("grp", "samp"), "snp"), P(("grp", "snp"), None)),
        out_specs=(
            P(("grp", "snp"), "samp", None, None),
            P("grp", None),
            P(("grp", "snp"), "samp", None, None),
        ),
        check_vma=False,
    )
```

```python
import functools

import jax
import jax.numpy as jnp
from jax import lax
from jax.experimental import pallas as pl
from jax.experimental.pallas import tpu as pltpu
from jax.sharding import PartitionSpec as P

PLANES = 6
STEPS = 64.0
TOP = 32767.0
BLOCK, LANES, SUB = 32, 128, 8
HIGH = lax.Precision.HIGHEST
VMEM_BYTES = 40 * 1024 * 1024


def params(**more):
    return pltpu.CompilerParams(vmem_limit_bytes=VMEM_BYTES, **more)


def planes_of(words):
    return [
        jnp.bitwise_and(jnp.right_shift(words, 2 * t), 3).astype(jnp.float32).astype(jnp.bfloat16)
        for t in range(PLANES)
    ]


def project_kernel(pick, words, basis, out, sums):
    blocks, _, depth, _ = out.shape
    total = jnp.zeros(sums.shape, jnp.float32)
    for t, plane in enumerate(planes_of(words[...])):
        product = jnp.dot(plane, basis[...], preferred_element_type=jnp.float32)
        for b in range(blocks):
            out[b, t] = product[b * depth : (b + 1) * depth]
        total = total + product.reshape(-1, 8, product.shape[1]).sum(axis=0)
    sums[...] = total


def project(words, basis, pick, blocks):
    count, snps = words.shape
    width = basis.shape[1]
    half = count // 2
    depth = half // blocks
    return pl.pallas_call(
        project_kernel,
        grid_spec=pltpu.PrefetchScalarGridSpec(
            num_scalar_prefetch=1,
            grid=(1,),
            in_specs=[
                pl.BlockSpec((half, snps), lambda i, pick: (pick[0], 0)),
                pl.BlockSpec((snps, width), lambda i, pick: (0, 0)),
            ],
            out_specs=[
                pl.BlockSpec((blocks, PLANES, depth, width), lambda i, pick: (0, 0, 0, 0)),
                pl.BlockSpec((8, width), lambda i, pick: (0, 0)),
            ],
        ),
        out_shape=[
            jax.ShapeDtypeStruct((blocks, PLANES, depth, width), jnp.float32),
            jax.ShapeDtypeStruct((8, width), jnp.float32),
        ],
        compiler_params=params(),
        name="project",
        cost_estimate=pl.CostEstimate(
            flops=2 * half * PLANES * snps * width,
            bytes_accessed=4 * half * snps + 2 * snps * width + 4 * half * PLANES * width,
            transcendentals=0,
        ),
    )(pick, words, basis)


def bit_reverse(index, bits):
    out = 0
    for b in range(bits):
        out |= ((index >> b) & 1) << (bits - 1 - b)
    return out


def back_project(words, scores, scale):
    blocks = scores.shape[0]
    bits = blocks.bit_length() - 1
    total = None
    for t, plane in enumerate(planes_of(words)):
        rows = jnp.concatenate([scores[bit_reverse(b, bits), t] for b in range(blocks)], axis=0)
        term = lax.dot_general(
            rows, plane, (((0,), (0,)), ((), ())), preferred_element_type=jnp.float32
        )
        total = term if total is None else total + term
    return (total * scale).T


def sent_kernel(scale, pick, words, scores, out):
    value = back_project(words[...], scores, scale)
    rows = value.shape[0]
    top = jnp.maximum(jnp.max(jnp.abs(value), axis=0, keepdims=True), 1e-30)
    level = jnp.ceil(STEPS * jnp.log2(top / TOP)) + 1.0
    unit = jnp.exp2(level * (1.0 / STEPS))
    coded = jnp.clip(jnp.round(value * (1.0 / unit)), -TOP, TOP)
    out[:rows] = coded.astype(jnp.int32).astype(jnp.int16)
    out[rows:] = jnp.broadcast_to(level, (16, level.shape[1])).astype(jnp.int32).astype(jnp.int16)


def kept_kernel(scale, pick, words, scores, out):
    out[...] = back_project(words[...], scores, scale)


def chunk_of_y(words, scores, pick, rows, scale, sent):
    count, snps = words.shape
    width = scores.shape[-1]
    shape = (rows + 16, width) if sent else (rows, width)
    dtype = jnp.int16 if sent else jnp.float32
    return pl.pallas_call(
        functools.partial(sent_kernel if sent else kept_kernel, scale),
        grid_spec=pltpu.PrefetchScalarGridSpec(
            num_scalar_prefetch=1,
            grid=(1,),
            in_specs=[
                pl.BlockSpec((count, rows), lambda i, pick: (0, pick[0])),
                pl.BlockSpec(scores.shape, lambda i, pick: (0, 0, 0, 0)),
            ],
            out_specs=pl.BlockSpec(shape, lambda i, pick: (0, 0)),
        ),
        out_shape=jax.ShapeDtypeStruct(shape, dtype),
        compiler_params=params(),
        name="chunk_sent" if sent else "chunk_kept",
        cost_estimate=pl.CostEstimate(
            flops=2 * count * PLANES * rows * width,
            bytes_accessed=4 * count * rows + 2 * scores.size + 4 * rows * width,
            transcendentals=0,
        ),
    )(pick, words, scores)


def collect_kernel(scale, *refs):
    kept, out, gram = refs[0], refs[-2], refs[-1]
    rows = kept.shape[0]
    total = kept[...]
    for ref in refs[1:-2]:
        level = ref[rows : rows + 16].astype(jnp.int32).astype(jnp.float32)[:1]
        unit = jnp.exp2(level * (1.0 / STEPS))
        total = total + ref[:rows].astype(jnp.int32).astype(jnp.float32) * unit
    out[...] = total
    gram[...] = scale * lax.dot_general(
        total, total, (((0,), (0,)), ((), ())), precision=HIGH, preferred_element_type=jnp.float32
    )


def collect(kept, received, scale):
    width = kept.shape[1]
    return pl.pallas_call(
        functools.partial(collect_kernel, scale),
        out_shape=[
            jax.ShapeDtypeStruct(kept.shape, jnp.float32),
            jax.ShapeDtypeStruct((width, width), jnp.float32),
        ],
        compiler_params=params(),
        name="collect",
    )(kept, *received)


def pieces(x):
    high = x.astype(jnp.bfloat16)
    rest = x - high.astype(jnp.float32)
    mid = rest.astype(jnp.bfloat16)
    low = (rest - mid.astype(jnp.float32)).astype(jnp.bfloat16)
    return high, mid, low

def factor(table, r_out):
    width = table.shape[0]
    tiles = width // LANES
    lane = lax.broadcasted_iota(jnp.int32, (SUB, LANES), 1)
    sub = lax.broadcasted_iota(jnp.int32, (SUB, LANES), 0)
    spread = lambda x, k: jnp.broadcast_to(x[k : k + 1], (SUB, LANES))
    for base in range(0, width, BLOCK):
        t, off = base // LANES, base % LANES
        groups = BLOCK // SUB
        rows = [
            [
                table[base + SUB * q : base + SUB * (q + 1), LANES * i : LANES * (i + 1)]
                for i in range(tiles)
            ]
            for q in range(groups)
        ]
        for p in range(groups):
            first = off + SUB * p
            cols = [
                [
                    jnp.broadcast_to(rows[q][t][:, first + m : first + m + 1], (SUB, LANES))
                    if q >= p
                    else None
                    for q in range(groups)
                ]
                for m in range(SUB)
            ]
            upper = rows[p][t]
            inside = (lane >= first) & (lane < first + SUB)
            unit = jnp.where(lane - first == sub, 1.0, 0.0)
            for q in range(p, groups):
                rows[q][t] = jnp.where(inside, unit if q == p else 0.0, rows[q][t])
            pivots = jnp.ones((SUB, LANES), jnp.float32)
            for k in range(SUB):
                pivot = spread(cols[k][p], k)
                inverse = 1.0 / pivot
                pivots = jnp.where(sub == k, pivot, pivots)
                step = [None] * groups
                for q in range(p, groups):
                    step[q] = (jnp.where(sub > k, cols[k][q], 0.0) if q == p else cols[k][q]) * inverse
                for m in range(k + 1, SUB):
                    line = spread(cols[m][p], k)
                    for q in range(p, groups):
                        cols[m][q] = cols[m][q] - step[q] * line
                for i in range(tiles):
                    line = spread(rows[p][i], k)
                    for q in range(p, groups):
                        rows[q][i] = rows[q][i] - step[q] * line
                upper = upper - step[p] * spread(upper, k)
            scale = lax.rsqrt(pivots)
            for i in range(tiles):
                rows[p][i] = rows[p][i] * scale
            upper = jnp.where(lane >= first + SUB, rows[p][t], upper * scale)
            upper = jnp.where(lane >= first + sub, upper, 0.0)
            place = slice(base + SUB * p, base + SUB * (p + 1))
            for i in range(tiles):
                r_out[place, LANES * i : LANES * (i + 1)] = (
                    upper if i == t else rows[p][i] if i > t else jnp.zeros((SUB, LANES), jnp.float32)
                )
        for p in range(groups - 1):
            rows[p][t] = jnp.where((lane >= off + SUB * (p + 1)) & (lane < off + BLOCK), 0.0, rows[p][t])
        whole = jnp.concatenate([jnp.concatenate(r, axis=1) for r in rows], axis=0)
        column = lax.broadcasted_iota(jnp.int32, (BLOCK, width), 1)
        table[base : base + BLOCK, :] = jnp.where(column < base + BLOCK, whole, 0.0)
        end = base + BLOCK
        if end < width:
            begin = end // LANES * LANES
            h, m, l = pieces(whole)
            left = jnp.concatenate([h, h, h, m, m, l], axis=0)[:, begin:]
            right = jnp.concatenate([h, m, l, h, m, h], axis=0)
            change = lax.dot_general(left, right, (((0,), (0,)), ((), ())), preferred_element_type=jnp.float32)
            column = lax.broadcasted_iota(jnp.int32, (width - end, width), 1)
            keep = jnp.where((column >= base) & (column < end), 0.0, table[end:, :])
            table[end:, :] = keep - change[end - begin :]

def basis_kernel(gram, y, r_out, q_out, table):
    table[...] = gram[...]
    factor(table, r_out)
    q_out[...] = lax.dot_general(
        y[...],
        table[...],
        (((1,), (1,)), ((), ())),
        precision=HIGH,
        preferred_element_type=jnp.float32,
    )


def orthonormalize(gram, y):
    width = gram.shape[0]
    return pl.pallas_call(
        basis_kernel,
        out_shape=[
            jax.ShapeDtypeStruct((width, width), jnp.float32),
            jax.ShapeDtypeStruct(y.shape, jnp.float32),
        ],
        scratch_shapes=[pltpu.VMEM((width, width), jnp.float32)],
        compiler_params=params(),
        name="orthonormalize",
    )(gram, y)


def swap(array, axis, mask):
    size = lax.axis_size(axis)
    return lax.ppermute(array, axis, [(i, i ^ mask) for i in range(size)])


def halve(array, axis, mask):
    bit = (lax.axis_index(axis) & mask) // mask
    mine = lax.dynamic_index_in_dim(array, bit, 0, keepdims=False)
    other = lax.dynamic_index_in_dim(array, 1 - bit, 0, keepdims=False)
    return mine, swap(other, axis, mask)


def gram_total(gram):
    width = gram.shape[0]
    n_snp, n_samp = lax.axis_size("snp"), lax.axis_size("samp")
    if n_snp != 4 or n_samp != 4:
        return lax.psum(gram, ("samp", "snp"))
    mine, got = halve(gram.reshape(2, width // 2, width), "snp", 1)
    part = mine + got
    mine, got = halve(part.reshape(2, width // 4, width), "snp", 2)
    part = mine + got
    part = ((part + swap(part, "samp", 1)) + (swap(part, "samp", 2) + swap(part, "samp", 3)))
    x_bit = (lax.axis_index("snp") // 2) == 0
    c_bit = (lax.axis_index("snp") % 2) == 0
    got = swap(part, "snp", 2)
    part = jnp.concatenate([jnp.where(x_bit, part, got), jnp.where(x_bit, got, part)], axis=0)
    got = swap(part, "snp", 1)
    return jnp.concatenate([jnp.where(c_bit, part, got), jnp.where(c_bit, got, part)], axis=0)


def per_device(genotypes, basis_cols):
    n_snp, n_samp = lax.axis_size("snp"), lax.axis_size("samp")
    bits = n_snp.bit_length() - 1
    words, snps = genotypes.shape
    width = basis_cols.shape[1]
    samples = words * PLANES * n_samp
    inv_root = float(1.0 / samples**0.5)
    blocks = n_snp // 2
    depth = words // n_snp
    me = lax.axis_index("snp")
    low = (me & 1).astype(jnp.int32)

    other, other_sums = project(genotypes, basis_cols, (1 - low)[None], blocks)
    got = swap(other, "snp", 1)
    mine, mine_sums = project(genotypes, basis_cols, low[None], blocks)
    part = mine + got
    sums = mine_sums + other_sums
    for b in range(1, bits):
        shape = (2, part.shape[0] // 2) + part.shape[1:]
        keep, got = halve(part.reshape(shape), "snp", 1 << b)
        part = keep + got
    if n_snp * n_samp <= 16:
        every = jnp.broadcast_to(sums[None], (n_snp * n_samp,) + sums.shape)
        center = lax.all_to_all(every, ("samp", "snp"), 0, 0, tiled=True).sum(axis=(0, 1))
    else:
        center = lax.psum(sums, ("samp", "snp")).sum(axis=0)
    center = center / jnp.float32(samples)
    rows = (part.reshape(PLANES * depth, width) - center[None, :]).astype(jnp.bfloat16)
    scores = lax.all_gather(rows, "snp").reshape(n_snp, PLANES, depth, width)

    chunk = snps // n_samp
    z = lax.axis_index("samp").astype(jnp.int32)
    total_snps = snps * n_snp
    if n_samp <= 4 and chunk % 128 == 0:
        received = []
        for mask in range(n_samp - 1, 0, -1):
            coded = chunk_of_y(genotypes, scores, (z ^ mask)[None], chunk, inv_root, True)
            received.append(swap(coded, "samp", mask))
        kept = chunk_of_y(genotypes, scores, z[None], chunk, inv_root, False)
        y_local, gram = collect(kept, received, 1.0 / total_snps)
    else:
        tile = 512 if snps % 512 == 0 else snps
        parts = [
            chunk_of_y(genotypes, scores, jnp.full((1,), i, jnp.int32), tile, inv_root, False)
            for i in range(snps // tile)
        ]
        y_local = lax.psum_scatter(
            jnp.concatenate(parts, axis=0), "samp", scatter_dimension=0, tiled=True
        )
        y_local, gram = collect(y_local, [], 1.0 / total_snps)
    gram_sum = gram_total(gram)
    r_factor, q_next = orthonormalize(gram_sum, y_local)
    layout = (1, 1, y_local.shape[0], width)
    return (y_local.reshape(layout), r_factor, q_next.reshape(layout))


def solution(mesh):
    return jax.shard_map(
        per_device,
        mesh=mesh,
        in_specs=(P(("grp", "samp"), "snp"), P(("grp", "snp"), None)),
        out_specs=(
            P(("grp", "snp"), "samp", None, None),
            P("grp", None),
            P(("grp", "snp"), "samp", None, None),
        ),
        check_vma=False,
    )
```

```python
import functools
import math

import jax
import jax.numpy as jnp
from jax import lax
from jax.experimental import pallas as pl
from jax.experimental.pallas import tpu as pltpu
from jax.sharding import PartitionSpec as P

PLANES = 6
STEPS = 64.0
TOP = 32767.0
BLOCK, LANES, SUB, PAD = 32, 128, 8, 32
HIGH = lax.Precision.HIGHEST
PAIRS = 0x333
VMEM_BYTES = 40 * 1024 * 1024


def params(**more):
    return pltpu.CompilerParams(vmem_limit_bytes=VMEM_BYTES, **more)


def planes_of(words):
    return [
        jnp.bitwise_and(jnp.right_shift(words, 2 * t), 3).astype(jnp.float32).astype(jnp.bfloat16)
        for t in range(PLANES)
    ]


def half_rows(words, basis, out, place):
    half = words.shape[0] // 2
    blocks, _, depth, _ = out.shape
    part = words[pl.ds(pl.multiple_of(place * half, half), half)]
    for t, plane in enumerate(planes_of(part)):
        product = jnp.dot(plane, basis[...], preferred_element_type=jnp.float32)
        for b in range(blocks):
            out[b, t] = product[b * depth : (b + 1) * depth]


def low_bit():
    return jnp.bitwise_and(lax.axis_index("snp"), 1)


def counts_of(words):
    total = None
    groups = words.shape[0] // 8
    for first in range(0, groups, 3):
        held = None
        for g in range(first, min(first + 3, groups)):
            word = words[8 * g : 8 * g + 8]
            pair = (word & PAIRS) + (jnp.right_shift(word, 2) & PAIRS)
            held = pair if held is None else held + pair
        held = (held & 15) + (jnp.right_shift(held, 4) & 15) + jnp.right_shift(held, 8)
        total = held if total is None else total + held
    return total


def other_kernel(words, basis, out, sums):
    counts = counts_of(words)
    pieces_ = jnp.concatenate([jnp.right_shift(counts, 4), counts & 15], axis=0)
    both_ = jnp.dot(
        pieces_.astype(jnp.float32).astype(jnp.bfloat16),
        basis[...],
        preferred_element_type=jnp.float32,
    )
    sums[...] = 16.0 * both_[:8] + both_[8:]
    half_rows(words, basis, out, 1 - low_bit())


def mine_kernel(words, basis, out):
    half_rows(words, basis, out, low_bit())


def project(words, basis, blocks, other):
    count, snps = words.shape
    width = basis.shape[1]
    half = count // 2
    shapes = [jax.ShapeDtypeStruct((blocks, PLANES, half // blocks, width), jnp.float32)]
    if other:
        shapes.append(jax.ShapeDtypeStruct((8, width), jnp.float32))
    return pl.pallas_call(
        other_kernel if other else mine_kernel,
        out_shape=shapes,
        compiler_params=params(),
        name="project_other" if other else "project_mine",
        cost_estimate=pl.CostEstimate(
            flops=2 * half * PLANES * snps * width,
            bytes_accessed=4 * half * snps + 2 * snps * width + 4 * half * PLANES * width,
            transcendentals=0,
        ),
    )(words, basis)


def merge_kernel(shift, mine, got, sums, more, send, keep, total):
    half = send.shape[0]
    bit = jnp.bitwise_and(jnp.right_shift(lax.axis_index("snp"), shift), 1)
    for b in range(half):
        for out, first in ((send, 1 - bit), (keep, bit)):
            out[b] = mine[first * half + b] + got[first * half + b]
    total[...] = sums[...] + more[...]


def merge(mine, got, shift, sums, more):
    half = (mine.shape[0] // 2,) + mine.shape[1:]
    return pl.pallas_call(
        functools.partial(merge_kernel, shift),
        out_shape=[jax.ShapeDtypeStruct(half, jnp.float32)] * 2
        + [jax.ShapeDtypeStruct(sums.shape, jnp.float32)],
        compiler_params=params(),
        name="merge",
    )(mine, got, sums, more)


def finish_kernel(samples, mine, got, sums, out):
    center = jnp.sum(sums[...], axis=0, keepdims=True) / jnp.float32(samples)
    value = (mine[...] + got[...]).reshape(out.shape) - center
    out[...] = value.astype(jnp.bfloat16)


def finish(mine, got, sums, samples):
    rows, width = mine.size // mine.shape[-1], mine.shape[-1]
    return pl.pallas_call(
        functools.partial(finish_kernel, samples),
        out_shape=jax.ShapeDtypeStruct((rows, width), jnp.bfloat16),
        compiler_params=params(),
        name="finish",
    )(mine, got, sums)


def bit_reverse(index, bits):
    out = 0
    for b in range(bits):
        out |= ((index >> b) & 1) << (bits - 1 - b)
    return out


def back_project(words, scores, scale):
    blocks = scores.shape[0]
    bits = blocks.bit_length() - 1
    total = None
    for t, plane in enumerate(planes_of(words)):
        rows = jnp.concatenate([scores[bit_reverse(b, bits), t] for b in range(blocks)], axis=0)
        term = lax.dot_general(
            rows, plane, (((0,), (0,)), ((), ())), preferred_element_type=jnp.float32
        )
        total = term if total is None else total + term
    return (total * scale).T


def chunk_value(scale, mask, piece, words, scores, rows):
    index = piece if mask is None else jnp.bitwise_xor(lax.axis_index("samp"), mask)
    span = pl.ds(pl.multiple_of(index * rows, rows), rows)
    return back_project(words[:, span], scores, scale)


def sent_kernel(scale, mask, words, scores, out):
    rows = out.shape[0] - 16
    value = chunk_value(scale, mask, 0, words, scores, rows)
    top = jnp.maximum(jnp.max(jnp.abs(value), axis=0, keepdims=True), 1e-30)
    level = jnp.ceil(STEPS * jnp.log2(top / TOP)) + 1.0
    unit = jnp.exp2(level * (1.0 / STEPS))
    coded = jnp.clip(jnp.round(value * (1.0 / unit)), -TOP, TOP)
    out[:rows] = coded.astype(jnp.int32).astype(jnp.int16)
    out[rows:] = jnp.broadcast_to(level, (16, level.shape[1])).astype(jnp.int32).astype(jnp.int16)


def kept_kernel(scale, mask, piece, words, scores, out):
    out[...] = chunk_value(scale, mask, piece, words, scores, out.shape[0])


def chunk_of_y(words, scores, rows, scale, mask, piece=0):
    width = scores.shape[-1]
    sent = mask is not None and mask > 0
    shape = (rows + 16, width) if sent else (rows, width)
    dtype = jnp.int16 if sent else jnp.float32
    kernel = functools.partial(sent_kernel, scale, mask)
    if not sent:
        kernel = functools.partial(kept_kernel, scale, mask, piece)
    return pl.pallas_call(
        kernel,
        out_shape=jax.ShapeDtypeStruct(shape, dtype),
        compiler_params=params(),
        name="chunk_sent" if sent else "chunk_kept",
        cost_estimate=pl.CostEstimate(
            flops=2 * words.shape[0] * PLANES * rows * width,
            bytes_accessed=4 * words.shape[0] * rows + 2 * scores.size + 4 * rows * width,
            transcendentals=0,
        ),
    )(words, scores)


def decoded(coded, rows):
    level = coded[rows : rows + 16].astype(jnp.int32).astype(jnp.float32)[:1]
    return coded[:rows].astype(jnp.int32).astype(jnp.float32) * jnp.exp2(level * (1.0 / STEPS))


def add_kernel(kept, coded, out):
    out[...] = kept[...] + decoded(coded, kept.shape[0])


def add_chunk(kept, coded):
    return pl.pallas_call(
        add_kernel,
        out_shape=jax.ShapeDtypeStruct(kept.shape, jnp.float32),
        compiler_params=params(),
        name="add_chunk",
        cost_estimate=pl.CostEstimate(
            flops=4 * kept.size, bytes_accessed=10 * kept.size, transcendentals=0
        ),
    )(kept, coded)


def pieces(x):
    high = x.astype(jnp.bfloat16)
    rest = x - high.astype(jnp.float32)
    mid = rest.astype(jnp.bfloat16)
    low = (rest - mid.astype(jnp.float32)).astype(jnp.bfloat16)
    return high, mid, low

def gram_blocks(total):
    high, mid, low = pieces(total)
    rows = (((0,), (0,)), ((), ()))
    product = functools.partial(
        lax.dot_general, dimension_numbers=rows, preferred_element_type=jnp.float32
    )
    small = product(high, mid) + product(high, low)
    whole = product(high, high) + (product(mid, mid) + (small + small.T))
    return whole[:LANES, :LANES], whole[:LANES, LANES:], whole[LANES:, LANES:]


def collect_kernel(scale, *refs):
    kept, out, copy, gram = refs[0], refs[-3], refs[-2], refs[-1]
    total = kept[...]
    for ref in refs[1:-3]:
        total = total + decoded(ref, kept.shape[0])
    out[...] = total
    copy[...] = total
    first, corner, second = (scale * block for block in gram_blocks(total))

    row = lax.broadcasted_iota(jnp.int32, first.shape, 0)
    column = lax.broadcasted_iota(jnp.int32, first.shape, 1)
    gram[:LANES] = jnp.where(row <= column, first, second)
    gram[LANES : 2 * LANES] = corner
    gram[2 * LANES :] = jnp.zeros((PAD, LANES), jnp.float32)
    gram[2 * LANES : 2 * LANES + 1] = jnp.sum(
        jnp.where(row == column, second, 0.0), axis=0, keepdims=True
    )


def unpack_gram(packed, table):
    mixed = packed[:LANES]
    turned = mixed.T
    row = lax.broadcasted_iota(jnp.int32, mixed.shape, 0)
    column = lax.broadcasted_iota(jnp.int32, mixed.shape, 1)
    table[:LANES, :LANES] = jnp.where(row <= column, mixed, turned)
    second = jnp.where(row > column, mixed, turned)
    table[LANES:, LANES:] = jnp.where(row == column, packed[2 * LANES : 2 * LANES + 1], second)
    table[:LANES, LANES:] = packed[LANES : 2 * LANES]
    table[LANES:, :LANES] = jnp.zeros((LANES, LANES), jnp.float32)


def collect(kept, received, scale):
    width = kept.shape[1]
    return pl.pallas_call(
        functools.partial(collect_kernel, scale),
        out_shape=[
            jax.ShapeDtypeStruct(kept.shape, jnp.float32),
            jax.ShapeDtypeStruct(kept.shape, jnp.float32),
            jax.ShapeDtypeStruct((width + PAD, LANES), jnp.float32),
        ],
        compiler_params=params(),
        name="collect",
    )(kept, *received)


def factor(table, r_out):
    width = table.shape[0]
    tiles = width // LANES
    lane = lax.broadcasted_iota(jnp.int32, (SUB, LANES), 1)
    sub = lax.broadcasted_iota(jnp.int32, (SUB, LANES), 0)
    spread = lambda x, k: jnp.broadcast_to(x[k : k + 1], (SUB, LANES))
    for base in range(0, width, BLOCK):
        t, off = base // LANES, base % LANES
        groups = BLOCK // SUB
        rows = [
            [
                table[base + SUB * q : base + SUB * (q + 1), LANES * i : LANES * (i + 1)]
                for i in range(tiles)
            ]
            for q in range(groups)
        ]
        for p in range(groups):
            first = off + SUB * p
            cols = [
                [
                    jnp.broadcast_to(rows[q][t][:, first + m : first + m + 1], (SUB, LANES))
                    if q >= p
                    else None
                    for q in range(groups)
                ]
                for m in range(SUB)
            ]
            upper = rows[p][t]
            inside = (lane >= first) & (lane < first + SUB)
            unit = jnp.where(lane - first == sub, 1.0, 0.0)
            for q in range(p, groups):
                rows[q][t] = jnp.where(inside, unit if q == p else 0.0, rows[q][t])
            pivots = jnp.ones((SUB, LANES), jnp.float32)
            for k in range(SUB):
                pivot = spread(cols[k][p], k)
                inverse = 1.0 / pivot
                pivots = jnp.where(sub == k, pivot, pivots)
                step = [None] * groups
                for q in range(p, groups):
                    step[q] = (jnp.where(sub > k, cols[k][q], 0.0) if q == p else cols[k][q]) * inverse
                for m in range(k + 1, SUB):
                    line = spread(cols[m][p], k)
                    for q in range(p, groups):
                        cols[m][q] = cols[m][q] - step[q] * line
                for i in range(tiles):
                    line = spread(rows[p][i], k)
                    for q in range(p, groups):
                        rows[q][i] = rows[q][i] - step[q] * line
                upper = upper - step[p] * spread(upper, k)
            scale = lax.rsqrt(pivots)
            for i in range(tiles):
                rows[p][i] = rows[p][i] * scale
            upper = jnp.where(lane >= first + SUB, rows[p][t], upper * scale)
            upper = jnp.where(lane >= first + sub, upper, 0.0)
            place = slice(base + SUB * p, base + SUB * (p + 1))
            for i in range(tiles):
                r_out[place, LANES * i : LANES * (i + 1)] = (
                    upper if i == t else rows[p][i] if i > t else jnp.zeros((SUB, LANES), jnp.float32)
                )
        for p in range(groups - 1):
            rows[p][t] = jnp.where((lane >= off + SUB * (p + 1)) & (lane < off + BLOCK), 0.0, rows[p][t])
        whole = jnp.concatenate([jnp.concatenate(r, axis=1) for r in rows], axis=0)
        column = lax.broadcasted_iota(jnp.int32, (BLOCK, width), 1)
        table[base : base + BLOCK, :] = jnp.where(column < base + BLOCK, whole, 0.0)
        end = base + BLOCK
        if end < width:
            begin = end // LANES * LANES
            h, m, l = pieces(whole)
            left = jnp.concatenate([h, h, h, m, m, l], axis=0)[:, begin:]
            right = jnp.concatenate([h, m, l, h, m, h], axis=0)
            change = lax.dot_general(left, right, (((0,), (0,)), ((), ())), preferred_element_type=jnp.float32)
            column = lax.broadcasted_iota(jnp.int32, (width - end, width), 1)
            keep = jnp.where((column >= base) & (column < end), 0.0, table[end:, :])
            table[end:, :] = keep - change[end - begin :]

def basis_kernel(gram, y, r_out, q_out, table):
    unpack_gram(gram, table)
    factor(table, r_out)
    q_out[...] = lax.dot_general(
        y[...],
        table[...],
        (((1,), (1,)), ((), ())),
        precision=HIGH,
        preferred_element_type=jnp.float32,
    )


def orthonormalize(gram, y):
    width = y.shape[1]
    return pl.pallas_call(
        basis_kernel,
        out_shape=[
            jax.ShapeDtypeStruct((width, width), jnp.float32),
            jax.ShapeDtypeStruct(y.shape, jnp.float32),
        ],
        scratch_shapes=[pltpu.VMEM((width, width), jnp.float32)],
        compiler_params=params(),
        name="orthonormalize",
    )(gram, y)


def swap(array, axis, mask):
    size = math.prod(lax.axis_size(name) for name in (axis if isinstance(axis, tuple) else (axis,)))
    return lax.ppermute(array, axis, [(i, i ^ mask) for i in range(size)])


def halve(array, axis, mask):
    bit = (lax.axis_index(axis) & mask) // mask
    mine = lax.dynamic_index_in_dim(array, bit, 0, keepdims=False)
    other = lax.dynamic_index_in_dim(array, 1 - bit, 0, keepdims=False)
    return mine, swap(other, axis, mask)


def both(mine, got, first):
    return jnp.concatenate([jnp.where(first, mine, got), jnp.where(first, got, mine)], axis=0)


def gram_total(gram):
    rows, width = gram.shape
    if lax.axis_size("snp") != 4 or lax.axis_size("samp") != 4:
        return lax.psum(gram, ("samp", "snp"))
    mine, got = halve(gram.reshape(2, rows // 2, width), "snp", 1)
    part = mine + got
    part = part + swap(part, "snp", 2)
    part = (part + swap(part, "samp", 1)) + (swap(part, "samp", 2) + swap(part, "samp", 3))
    return both(part, swap(part, "snp", 1), jnp.bitwise_and(lax.axis_index("snp"), 1) == 0)


def per_device(genotypes, basis_cols):
    n_snp, n_samp = lax.axis_size("snp"), lax.axis_size("samp")
    bits = n_snp.bit_length() - 1
    words, snps = genotypes.shape
    width = basis_cols.shape[1]
    samples = words * PLANES * n_samp
    inv_root = float(1.0 / samples**0.5)
    blocks = n_snp // 2
    depth = words // n_snp

    other, sums = project(genotypes, basis_cols, blocks, True)
    if n_samp <= 4:
        more = swap(sums, "samp", 1)
    else:
        more = lax.psum(sums, "samp") - sums
    got = swap(other, "snp", 1)
    (mine,) = project(genotypes, basis_cols, blocks, False)
    for b in range(1, bits):
        send, mine, sums = merge(mine, got, b, sums, more)
        got = swap(send, "snp", 1 << b)
        more = jnp.zeros_like(sums)
    if n_samp <= 4:
        for b in range(1, n_samp.bit_length() - 1):
            sums = sums + swap(sums, "samp", 1 << b)
    for b in range(bits):
        sums = sums + swap(sums, "snp", 1 << b)
    rows = finish(mine, got, sums, samples)
    scores = lax.all_gather(rows, "snp").reshape(n_snp, PLANES, depth, width)

    chunk = snps // n_samp
    total_snps = snps * n_snp
    if n_samp <= 4 and chunk % 128 == 0:
        received = []
        for mask in range(n_samp - 1, 0, -1):
            coded = chunk_of_y(genotypes, scores, chunk, inv_root, mask)
            received.append(swap(coded, "samp", mask))
        kept = chunk_of_y(genotypes, scores, chunk, inv_root, 0)
        kept = add_chunk(kept, received[0])
        y_local, y_again, gram = collect(kept, received[1:], 1.0 / total_snps)
    else:
        tile = 512 if snps % 512 == 0 else snps
        parts = [
            chunk_of_y(genotypes, scores, tile, inv_root, None, i)
            for i in range(snps // tile)
        ]
        y_local = lax.psum_scatter(
            jnp.concatenate(parts, axis=0), "samp", scatter_dimension=0, tiled=True
        )
        y_local, y_again, gram = collect(y_local, [], 1.0 / total_snps)
    gram_sum = gram_total(gram)
    r_factor, q_next = orthonormalize(gram_sum, y_again)
    layout = (1, 1, y_local.shape[0], width)
    return (y_local.reshape(layout), r_factor, q_next.reshape(layout))


def solution(mesh):
    return jax.shard_map(
        per_device,
        mesh=mesh,
        in_specs=(P(("grp", "samp"), "snp"), P(("grp", "snp"), None)),
        out_specs=(
            P(("grp", "snp"), "samp", None, None),
            P("grp", None),
            P(("grp", "snp"), "samp", None, None),
        ),
        check_vma=False,
    )
```

```python
import functools
import math

import jax
import jax.numpy as jnp
from jax import lax
from jax.experimental import pallas as pl
from jax.experimental.pallas import tpu as pltpu
from jax.sharding import PartitionSpec as P

PLANES = 6
STEPS = 64.0
TOP = 32767.0
BLOCK, LANES, SUB, PAD = 32, 128, 8, 32
HIGH = lax.Precision.HIGHEST
PAIRS = 0x333
VMEM_BYTES = 40 * 1024 * 1024


def params(**more):
    return pltpu.CompilerParams(vmem_limit_bytes=VMEM_BYTES, **more)


def planes_of(words):
    return [
        jnp.bitwise_and(jnp.right_shift(words, 2 * t), 3).astype(jnp.float32).astype(jnp.bfloat16)
        for t in range(PLANES)
    ]


def half_rows(words, basis, out, place):
    half = words.shape[0] // 2
    part = words[pl.ds(pl.multiple_of(place * half, half), half)]
    for t, plane in enumerate(planes_of(part)):
        out[t] = jnp.dot(plane, basis[...], preferred_element_type=jnp.float32)


def low_bit():
    return jnp.bitwise_and(lax.axis_index("snp"), 1)


def counts_of(words):
    total = None
    groups = words.shape[0] // 8
    for first in range(0, groups, 3):
        held = None
        for g in range(first, min(first + 3, groups)):
            word = words[8 * g : 8 * g + 8]
            pair = (word & PAIRS) + (jnp.right_shift(word, 2) & PAIRS)
            held = pair if held is None else held + pair
        held = (held & 15) + (jnp.right_shift(held, 4) & 15) + jnp.right_shift(held, 8)
        total = held if total is None else total + held
    return total


def other_kernel(words, basis, out, sums):
    counts = counts_of(words)
    pieces_ = jnp.concatenate([jnp.right_shift(counts, 4), counts & 15], axis=0)
    both_ = jnp.dot(
        pieces_.astype(jnp.float32).astype(jnp.bfloat16),
        basis[...],
        preferred_element_type=jnp.float32,
    )
    sums[...] = 16.0 * both_[:8] + both_[8:]
    half_rows(words, basis, out, 1 - low_bit())


def mine_kernel(words, basis, out):
    half_rows(words, basis, out, low_bit())


def project(words, basis, other):
    count, snps = words.shape
    width = basis.shape[1]
    half = count // 2
    shapes = [jax.ShapeDtypeStruct((PLANES, half, width), jnp.float32)]
    if other:
        shapes.append(jax.ShapeDtypeStruct((8, width), jnp.float32))
    return pl.pallas_call(
        other_kernel if other else mine_kernel,
        out_shape=shapes,
        compiler_params=params(),
        name="project_other" if other else "project_mine",
        cost_estimate=pl.CostEstimate(
            flops=2 * half * PLANES * snps * width,
            bytes_accessed=4 * half * snps + 2 * snps * width + 4 * half * PLANES * width,
            transcendentals=0,
        ),
    )(words, basis)


def merge_kernel(mine, got, sums, more, *outs):
    span = outs[0].shape[-1]
    for i, out in enumerate(outs[:-1]):
        columns = slice(i * span, (i + 1) * span)
        out[...] = mine[:, :, columns] + got[:, :, columns]
    outs[-1][...] = sums[...] + more[...]


def merge(mine, got, sums, more, groups):
    shape = mine.shape[:2] + (mine.shape[2] // groups,)
    return pl.pallas_call(
        merge_kernel,
        out_shape=[jax.ShapeDtypeStruct(shape, jnp.float32)] * groups
        + [jax.ShapeDtypeStruct(sums.shape, jnp.float32)],
        compiler_params=params(),
        name="merge",
    )(mine, got, sums, more)


def finish_kernel(samples, group, mine, got, sums, out):
    span = out.shape[-1]
    columns = sums[:, group * span : (group + 1) * span]
    center = jnp.sum(columns, axis=0, keepdims=True) / jnp.float32(samples)
    out[...] = (mine[...] + got[...] - center[None]).astype(jnp.bfloat16)


def finish(mine, got, sums, samples, group):
    return pl.pallas_call(
        functools.partial(finish_kernel, samples, group),
        out_shape=jax.ShapeDtypeStruct(mine.shape, jnp.bfloat16),
        compiler_params=params(),
        name="finish",
    )(mine, got, sums)


def back_project(words, mine, other, scale):
    total = None
    for t, plane in enumerate(planes_of(words)):
        rows = jnp.concatenate([mine[t], other[t]], axis=0)
        term = lax.dot_general(
            rows, plane, (((0,), (0,)), ((), ())), preferred_element_type=jnp.float32
        )
        total = term if total is None else total + term
    return (total * scale).T


def chunk_value(scale, mask, piece, words, mine, other, rows):
    index = piece if mask is None else jnp.bitwise_xor(lax.axis_index("samp"), mask)
    span = pl.ds(pl.multiple_of(index * rows, rows), rows)
    half = words.shape[0] // 2
    first, second = (
        words[pl.ds(pl.multiple_of(place * half, half), half), span]
        for place in (low_bit(), 1 - low_bit())
    )
    return back_project(jnp.concatenate([first, second], axis=0), mine, other, scale)


def encode(value, out):
    rows = value.shape[0]
    top = jnp.maximum(jnp.max(jnp.abs(value), axis=0, keepdims=True), 1e-30)
    level = jnp.ceil(STEPS * jnp.log2(top / TOP)) + 1.0
    unit = jnp.exp2(level * (1.0 / STEPS))
    coded = jnp.clip(jnp.round(value * (1.0 / unit)), -TOP, TOP)
    out[:rows] = coded.astype(jnp.int32).astype(jnp.int16)
    out[rows:] = jnp.broadcast_to(level, (16, level.shape[1])).astype(jnp.int32).astype(jnp.int16)


def chunks_kernel(scale, masks, rows, words, mine, other, *outs):
    for mask, out in zip(masks, outs):
        value = chunk_value(scale, mask, 0, words, mine, other, rows)
        if mask:
            encode(value, out)
        else:
            out[...] = value


def piece_kernel(scale, piece, words, mine, other, out):
    out[...] = chunk_value(scale, None, piece, words, mine, other, out.shape[0])


def chunks_of_y(words, scores, rows, scale, masks=None, piece=None):
    width = scores[0].shape[-1]
    if masks is None:
        kernel = functools.partial(piece_kernel, scale, piece)
        shapes = [jax.ShapeDtypeStruct((rows, width), jnp.float32)]
    else:
        kernel = functools.partial(chunks_kernel, scale, masks, rows)
        shapes = [
            jax.ShapeDtypeStruct((rows + 16, width), jnp.int16)
            if mask
            else jax.ShapeDtypeStruct((rows, width), jnp.float32)
            for mask in masks
        ]
    return pl.pallas_call(
        kernel,
        out_shape=shapes,
        compiler_params=params(),
        name="chunks",
        cost_estimate=pl.CostEstimate(
            flops=2 * words.shape[0] * PLANES * rows * width * len(shapes),
            bytes_accessed=(4 * words.shape[0] + 4 * width) * rows * len(shapes),
            transcendentals=0,
        ),
    )(words, *scores)


def decoded(coded, rows):
    level = coded[rows : rows + 16].astype(jnp.int32).astype(jnp.float32)[:1]
    return coded[:rows].astype(jnp.int32).astype(jnp.float32) * jnp.exp2(level * (1.0 / STEPS))


def add_kernel(kept, *refs):
    total = kept[...]
    for ref in refs[:-1]:
        total = total + decoded(ref, kept.shape[0])
    refs[-1][...] = total


def add_chunks(kept, received):
    return pl.pallas_call(
        add_kernel,
        out_shape=jax.ShapeDtypeStruct(kept.shape, jnp.float32),
        compiler_params=params(),
        name="add_chunks",
        cost_estimate=pl.CostEstimate(
            flops=4 * kept.size, bytes_accessed=10 * kept.size, transcendentals=0
        ),
    )(kept, *received)


def pieces(x):
    high = x.astype(jnp.bfloat16)
    rest = x - high.astype(jnp.float32)
    mid = rest.astype(jnp.bfloat16)
    low = (rest - mid.astype(jnp.float32)).astype(jnp.bfloat16)
    return high, mid, low

def gram_blocks(total):
    high, mid, low = pieces(total)
    rows = (((0,), (0,)), ((), ()))
    product = functools.partial(
        lax.dot_general, dimension_numbers=rows, preferred_element_type=jnp.float32
    )
    small = product(high, mid) + product(high, low)
    whole = product(high, high) + (product(mid, mid) + (small + small.T))
    return whole[:LANES, :LANES], whole[:LANES, LANES:], whole[LANES:, LANES:]


def collect_kernel(scale, done, kept, *refs):
    out, copy, gram = refs[-3:]
    last = kept[...]
    for ref in refs[:-3]:
        last = last + decoded(ref, kept.shape[0])
    total = jnp.concatenate([done[...], last], axis=1)
    out[...] = total
    copy[...] = total
    first, corner, second = (scale * block for block in gram_blocks(total))

    row = lax.broadcasted_iota(jnp.int32, first.shape, 0)
    column = lax.broadcasted_iota(jnp.int32, first.shape, 1)
    gram[:LANES] = jnp.where(row <= column, first, second)
    gram[LANES : 2 * LANES] = corner
    gram[2 * LANES :] = jnp.zeros((PAD, LANES), jnp.float32)
    gram[2 * LANES : 2 * LANES + 1] = jnp.sum(
        jnp.where(row == column, second, 0.0), axis=0, keepdims=True
    )


def unpack_gram(packed, table):
    mixed = packed[:LANES]
    turned = mixed.T
    row = lax.broadcasted_iota(jnp.int32, mixed.shape, 0)
    column = lax.broadcasted_iota(jnp.int32, mixed.shape, 1)
    table[:LANES, :LANES] = jnp.where(row <= column, mixed, turned)
    second = jnp.where(row > column, mixed, turned)
    table[LANES:, LANES:] = jnp.where(row == column, packed[2 * LANES : 2 * LANES + 1], second)
    table[:LANES, LANES:] = packed[LANES : 2 * LANES]
    table[LANES:, :LANES] = jnp.zeros((LANES, LANES), jnp.float32)


def collect(done, kept, received, scale):
    rows, width = kept.shape[0], done.shape[1] + kept.shape[1]
    return pl.pallas_call(
        functools.partial(collect_kernel, scale),
        out_shape=[
            jax.ShapeDtypeStruct((rows, width), jnp.float32),
            jax.ShapeDtypeStruct((rows, width), jnp.float32),
            jax.ShapeDtypeStruct((width + PAD, LANES), jnp.float32),
        ],
        compiler_params=params(),
        name="collect",
    )(done, kept, *received)


def factor(table, r_out):
    width = table.shape[0]
    tiles = width // LANES
    lane = lax.broadcasted_iota(jnp.int32, (SUB, LANES), 1)
    sub = lax.broadcasted_iota(jnp.int32, (SUB, LANES), 0)
    spread = lambda x, k: jnp.broadcast_to(x[k : k + 1], (SUB, LANES))
    for base in range(0, width, BLOCK):
        t, off = base // LANES, base % LANES
        groups = BLOCK // SUB
        rows = [
            [
                table[base + SUB * q : base + SUB * (q + 1), LANES * i : LANES * (i + 1)]
                for i in range(tiles)
            ]
            for q in range(groups)
        ]
        for p in range(groups):
            first = off + SUB * p
            cols = [
                [
                    jnp.broadcast_to(rows[q][t][:, first + m : first + m + 1], (SUB, LANES))
                    if q >= p
                    else None
                    for q in range(groups)
                ]
                for m in range(SUB)
            ]
            upper = rows[p][t]
            inside = (lane >= first) & (lane < first + SUB)
            unit = jnp.where(lane - first == sub, 1.0, 0.0)
            for q in range(p, groups):
                rows[q][t] = jnp.where(inside, unit if q == p else 0.0, rows[q][t])
            pivots = jnp.ones((SUB, LANES), jnp.float32)
            for k in range(SUB):
                pivot = spread(cols[k][p], k)
                inverse = 1.0 / pivot
                pivots = jnp.where(sub == k, pivot, pivots)
                step = [None] * groups
                for q in range(p, groups):
                    step[q] = (jnp.where(sub > k, cols[k][q], 0.0) if q == p else cols[k][q]) * inverse
                for m in range(k + 1, SUB):
                    line = spread(cols[m][p], k)
                    for q in range(p, groups):
                        cols[m][q] = cols[m][q] - step[q] * line
                for i in range(tiles):
                    line = spread(rows[p][i], k)
                    for q in range(p, groups):
                        rows[q][i] = rows[q][i] - step[q] * line
                upper = upper - step[p] * spread(upper, k)
            scale = lax.rsqrt(pivots)
            for i in range(tiles):
                rows[p][i] = rows[p][i] * scale
            upper = jnp.where(lane >= first + SUB, rows[p][t], upper * scale)
            upper = jnp.where(lane >= first + sub, upper, 0.0)
            place = slice(base + SUB * p, base + SUB * (p + 1))
            for i in range(tiles):
                r_out[place, LANES * i : LANES * (i + 1)] = (
                    upper if i == t else rows[p][i] if i > t else jnp.zeros((SUB, LANES), jnp.float32)
                )
        for p in range(groups - 1):
            rows[p][t] = jnp.where((lane >= off + SUB * (p + 1)) & (lane < off + BLOCK), 0.0, rows[p][t])
        whole = jnp.concatenate([jnp.concatenate(r, axis=1) for r in rows], axis=0)
        column = lax.broadcasted_iota(jnp.int32, (BLOCK, width), 1)
        table[base : base + BLOCK, :] = jnp.where(column < base + BLOCK, whole, 0.0)
        end = base + BLOCK
        if end < width:
            begin = end // LANES * LANES
            h, m, l = pieces(whole)
            left = jnp.concatenate([h, h, h, m, m, l], axis=0)[:, begin:]
            right = jnp.concatenate([h, m, l, h, m, h], axis=0)
            change = lax.dot_general(left, right, (((0,), (0,)), ((), ())), preferred_element_type=jnp.float32)
            column = lax.broadcasted_iota(jnp.int32, (width - end, width), 1)
            keep = jnp.where((column >= base) & (column < end), 0.0, table[end:, :])
            table[end:, :] = keep - change[end - begin :]

def basis_kernel(gram, y, r_out, q_out, table):
    unpack_gram(gram, table)
    factor(table, r_out)
    q_out[...] = lax.dot_general(
        y[...],
        table[...],
        (((1,), (1,)), ((), ())),
        precision=HIGH,
        preferred_element_type=jnp.float32,
    )


def orthonormalize(gram, y):
    width = y.shape[1]
    return pl.pallas_call(
        basis_kernel,
        out_shape=[
            jax.ShapeDtypeStruct((width, width), jnp.float32),
            jax.ShapeDtypeStruct(y.shape, jnp.float32),
        ],
        scratch_shapes=[pltpu.VMEM((width, width), jnp.float32)],
        compiler_params=params(),
        name="orthonormalize",
    )(gram, y)


def swap(array, axis, mask):
    size = math.prod(lax.axis_size(name) for name in (axis if isinstance(axis, tuple) else (axis,)))
    return lax.ppermute(array, axis, [(i, i ^ mask) for i in range(size)])


def both(mine, got, first):
    return jnp.concatenate([jnp.where(first, mine, got), jnp.where(first, got, mine)], axis=0)


def gram_total(gram):
    rows, width = gram.shape
    if lax.axis_size("snp") != 4 or lax.axis_size("samp") != 4:
        return lax.psum(gram, ("samp", "snp"))
    bit = jnp.bitwise_and(lax.axis_index("snp"), 1)
    halves = gram.reshape(2, rows // 2, width)
    mine, other = (lax.dynamic_index_in_dim(halves, b, 0, keepdims=False) for b in (bit, 1 - bit))
    part = mine + swap(other, "snp", 1)
    part = part + swap(part, "snp", 2)
    part = (part + swap(part, "samp", 1)) + (swap(part, "samp", 2) + swap(part, "samp", 3))
    return both(part, swap(part, "snp", 1), bit == 0)


def per_device(genotypes, basis_cols):
    n_snp, n_samp = lax.axis_size("snp"), lax.axis_size("samp")
    bits = n_snp.bit_length() - 1
    words, snps = genotypes.shape
    width = basis_cols.shape[1]
    samples = words * PLANES * n_samp
    inv_root = float(1.0 / samples**0.5)
    chunk = snps // n_samp
    direct = n_samp <= 4 and chunk % LANES == 0

    other, sums = project(genotypes, basis_cols, True)
    got = swap(other, "snp", 1)
    if n_snp <= 4:
        more = sum(swap(sums, "snp", mask) for mask in range(1, n_snp))
    else:
        more = lax.psum(sums, "snp") - sums
    (mine,) = project(genotypes, basis_cols, False)
    *parts, sums = merge(mine, got, sums, more, 2)
    if n_samp <= 4:
        for b in range(n_samp.bit_length() - 1):
            sums = sums + swap(sums, "samp", 1 << b)
    else:
        sums = lax.psum(sums, "samp")

    kept, received = [], []
    got, sent = None, None
    for group, part in enumerate(parts):
        if got is not None:
            part, _, _ = lax.optimization_barrier((part, got, sums))
        for b in range(1, bits - 1):
            part = part + swap(part, "snp", 1 << b)
        got = swap(part, "snp", 1 << (bits - 1))
        ready = got
        if sent is not None:
            ready, _ = lax.optimization_barrier((got, sent[0]))
        rows = finish(part, ready, sums, samples, group)
        scores = (rows, swap(rows, "snp", 1))
        if direct:
            masks = (2, 1, 3)
            *coded, own = chunks_of_y(genotypes, scores, chunk, inv_root, masks + (0,))
            kept.append(own)
            received.append([swap(c, "samp", mask) for c, mask in zip(coded, masks)])
            sent = received[-1]
        else:
            tile = 4 * LANES if snps % (4 * LANES) == 0 else snps
            tiles = [
                chunks_of_y(genotypes, scores, tile, inv_root, piece=i)[0]
                for i in range(snps // tile)
            ]
            whole = jnp.concatenate(tiles, axis=0)
            kept.append(lax.psum_scatter(whole, "samp", scatter_dimension=0, tiled=True))
            received.append([])
    done = add_chunks(kept[0], received[0]) if direct else kept[0]
    y_local, y_again, gram = collect(done, kept[1], received[1], 1.0 / (snps * n_snp))
    gram_sum = gram_total(gram)
    r_factor, q_next = orthonormalize(gram_sum, y_again)
    layout = (1, 1, y_local.shape[0], width)
    return (y_local.reshape(layout), r_factor, q_next.reshape(layout))


def solution(mesh):
    return jax.shard_map(
        per_device,
        mesh=mesh,
        in_specs=(P(("grp", "samp"), "snp"), P(("grp", "snp"), None)),
        out_specs=(
            P(("grp", "snp"), "samp", None, None),
            P("grp", None),
            P(("grp", "snp"), "samp", None, None),
        ),
        check_vma=False,
    )
```

```python
import functools
import math

import jax
import jax.numpy as jnp
from jax import lax
from jax.experimental import pallas as pl
from jax.experimental.pallas import tpu as pltpu
from jax.sharding import PartitionSpec as P

PLANES = 6
STEPS = 64.0
TOP = 32767.0
BLOCK, LANES, SUB, PAD = 32, 128, 8, 32
HIGH = lax.Precision.HIGHEST
PAIRS = 0x333
VMEM_BYTES = 40 * 1024 * 1024


def params(**more):
    return pltpu.CompilerParams(vmem_limit_bytes=VMEM_BYTES, **more)


def planes_of(words):
    return [
        jnp.bitwise_and(jnp.right_shift(words, 2 * t), 3).astype(jnp.float32).astype(jnp.bfloat16)
        for t in range(PLANES)
    ]


def half_rows(words, basis, out, place):
    half = words.shape[0] // 2
    part = words[pl.ds(pl.multiple_of(place * half, half), half)]
    for t, plane in enumerate(planes_of(part)):
        out[t] = jnp.dot(plane, basis[...], preferred_element_type=jnp.float32)


def low_bit():
    return jnp.bitwise_and(lax.axis_index("snp"), 1)


def counts_of(words):
    total = None
    groups = words.shape[0] // 8
    for first in range(0, groups, 3):
        held = None
        for g in range(first, min(first + 3, groups)):
            word = words[8 * g : 8 * g + 8]
            pair = (word & PAIRS) + (jnp.right_shift(word, 2) & PAIRS)
            held = pair if held is None else held + pair
        held = (held & 15) + (jnp.right_shift(held, 4) & 15) + jnp.right_shift(held, 8)
        total = held if total is None else total + held
    return total


def other_kernel(words, basis, out, sums):
    counts = counts_of(words)
    pieces_ = jnp.concatenate([jnp.right_shift(counts, 4), counts & 15], axis=0)
    both_ = jnp.dot(
        pieces_.astype(jnp.float32).astype(jnp.bfloat16),
        basis[...],
        preferred_element_type=jnp.float32,
    )
    sums[...] = 16.0 * both_[:8] + both_[8:]
    half_rows(words, basis, out, 1 - low_bit())


def mine_kernel(words, basis, out):
    half_rows(words, basis, out, low_bit())


def project(words, basis, other):
    count, snps = words.shape
    width = basis.shape[1]
    half = count // 2
    shapes = [jax.ShapeDtypeStruct((PLANES, half, width), jnp.float32)]
    if other:
        shapes.append(jax.ShapeDtypeStruct((8, width), jnp.float32))
    return pl.pallas_call(
        other_kernel if other else mine_kernel,
        out_shape=shapes,
        compiler_params=params(),
        name="project_other" if other else "project_mine",
        cost_estimate=pl.CostEstimate(
            flops=2 * half * PLANES * snps * width,
            bytes_accessed=4 * half * snps + 2 * snps * width + 4 * half * PLANES * width,
            transcendentals=0,
        ),
    )(words, basis)


def merge_kernel(mine, got, sums, more, *outs):
    span = outs[0].shape[-1]
    for i, out in enumerate(outs[:-1]):
        columns = slice(i * span, (i + 1) * span)
        out[...] = mine[:, :, columns] + got[:, :, columns]
    outs[-1][...] = sums[...] + more[...]


def merge(mine, got, sums, more, groups):
    shape = mine.shape[:2] + (mine.shape[2] // groups,)
    return pl.pallas_call(
        merge_kernel,
        out_shape=[jax.ShapeDtypeStruct(shape, jnp.float32)] * groups
        + [jax.ShapeDtypeStruct(sums.shape, jnp.float32)],
        compiler_params=params(),
        name="merge",
    )(mine, got, sums, more)


def finish_kernel(samples, group, mine, got, sums, out):
    span = out.shape[-1]
    columns = sums[:, group * span : (group + 1) * span]
    center = jnp.sum(columns, axis=0, keepdims=True) / jnp.float32(samples)
    out[...] = (mine[...] + got[...] - center[None]).astype(jnp.bfloat16)


def finish(mine, got, sums, samples, group):
    return pl.pallas_call(
        functools.partial(finish_kernel, samples, group),
        out_shape=jax.ShapeDtypeStruct(mine.shape, jnp.bfloat16),
        compiler_params=params(),
        name="finish",
    )(mine, got, sums)


def back_project(words, mine, other, scale):
    total = None
    for t, plane in enumerate(planes_of(words)):
        rows = jnp.concatenate([mine[t], other[t]], axis=0)
        term = lax.dot_general(
            rows, plane, (((0,), (0,)), ((), ())), preferred_element_type=jnp.float32
        )
        total = term if total is None else total + term
    return (total * scale).T


def chunk_value(scale, mask, piece, words, mine, other, rows):
    index = piece if mask is None else jnp.bitwise_xor(lax.axis_index("samp"), mask)
    span = pl.ds(pl.multiple_of(index * rows, rows), rows)
    half = words.shape[0] // 2
    first, second = (
        words[pl.ds(pl.multiple_of(place * half, half), half), span]
        for place in (low_bit(), 1 - low_bit())
    )
    return back_project(jnp.concatenate([first, second], axis=0), mine, other, scale)


def encode(value, out):
    rows = value.shape[0]
    top = jnp.maximum(jnp.max(jnp.abs(value), axis=0, keepdims=True), 1e-30)
    level = jnp.ceil(STEPS * jnp.log2(top / TOP)) + 1.0
    unit = jnp.exp2(level * (1.0 / STEPS))
    coded = jnp.clip(jnp.round(value * (1.0 / unit)), -TOP, TOP)
    out[:rows] = coded.astype(jnp.int32).astype(jnp.int16)
    out[rows:] = jnp.broadcast_to(level, (16, level.shape[1])).astype(jnp.int32).astype(jnp.int16)


def chunks_kernel(scale, masks, rows, words, mine, other, *outs):
    for mask, out in zip(masks, outs):
        value = chunk_value(scale, mask, 0, words, mine, other, rows)
        if mask:
            encode(value, out)
        else:
            out[...] = value


def piece_kernel(scale, piece, words, mine, other, out):
    out[...] = chunk_value(scale, None, piece, words, mine, other, out.shape[0])


def chunks_of_y(words, scores, rows, scale, masks=None, piece=None):
    width = scores[0].shape[-1]
    if masks is None:
        kernel = functools.partial(piece_kernel, scale, piece)
        shapes = [jax.ShapeDtypeStruct((rows, width), jnp.float32)]
    else:
        kernel = functools.partial(chunks_kernel, scale, masks, rows)
        shapes = [
            jax.ShapeDtypeStruct((rows + 16, width), jnp.int16)
            if mask
            else jax.ShapeDtypeStruct((rows, width), jnp.float32)
            for mask in masks
        ]
    return pl.pallas_call(
        kernel,
        out_shape=shapes,
        compiler_params=params(),
        name="chunks",
        cost_estimate=pl.CostEstimate(
            flops=2 * words.shape[0] * PLANES * rows * width * len(shapes),
            bytes_accessed=(4 * words.shape[0] + 4 * width) * rows * len(shapes),
            transcendentals=0,
        ),
    )(words, *scores)


def decoded(coded, rows):
    level = coded[rows : rows + 16].astype(jnp.int32).astype(jnp.float32)[:1]
    return coded[:rows].astype(jnp.int32).astype(jnp.float32) * jnp.exp2(level * (1.0 / STEPS))


def add_kernel(kept, *refs):
    total = kept[...]
    for ref in refs[:-1]:
        total = total + decoded(ref, kept.shape[0])
    refs[-1][...] = total


def add_chunks(kept, received):
    return pl.pallas_call(
        add_kernel,
        out_shape=jax.ShapeDtypeStruct(kept.shape, jnp.float32),
        compiler_params=params(),
        name="add_chunks",
        cost_estimate=pl.CostEstimate(
            flops=4 * kept.size, bytes_accessed=10 * kept.size, transcendentals=0
        ),
    )(kept, *received)


def pieces(x):
    high = x.astype(jnp.bfloat16)
    rest = x - high.astype(jnp.float32)
    mid = rest.astype(jnp.bfloat16)
    low = (rest - mid.astype(jnp.float32)).astype(jnp.bfloat16)
    return high, mid, low

def gram_blocks(total):
    high, mid, low = pieces(total)
    rows = (((0,), (0,)), ((), ()))
    product = functools.partial(
        lax.dot_general, dimension_numbers=rows, preferred_element_type=jnp.float32
    )
    small = product(high, mid) + product(high, low)
    whole = product(high, high) + (product(mid, mid) + (small + small.T))
    return whole[:LANES, :LANES], whole[:LANES, LANES:], whole[LANES:, LANES:]


def collect_kernel(scale, done, kept, *refs):
    out, copy, gram = refs[-3:]
    last = kept[...]
    for ref in refs[:-3]:
        last = last + decoded(ref, kept.shape[0])
    total = jnp.concatenate([done[...], last], axis=1)
    out[...] = total
    copy[...] = total
    first, corner, second = (scale * block for block in gram_blocks(total))

    row = lax.broadcasted_iota(jnp.int32, first.shape, 0)
    column = lax.broadcasted_iota(jnp.int32, first.shape, 1)
    gram[:LANES] = jnp.where(row <= column, first, second)
    gram[LANES : 2 * LANES] = corner
    gram[2 * LANES :] = jnp.zeros((PAD, LANES), jnp.float32)
    gram[2 * LANES : 2 * LANES + 1] = jnp.sum(
        jnp.where(row == column, second, 0.0), axis=0, keepdims=True
    )


def unpack_gram(packed, table):
    mixed = packed[:LANES]
    turned = mixed.T
    row = lax.broadcasted_iota(jnp.int32, mixed.shape, 0)
    column = lax.broadcasted_iota(jnp.int32, mixed.shape, 1)
    table[:LANES, :LANES] = jnp.where(row <= column, mixed, turned)
    second = jnp.where(row > column, mixed, turned)
    table[LANES:, LANES:] = jnp.where(row == column, packed[2 * LANES : 2 * LANES + 1], second)
    table[:LANES, LANES:] = packed[LANES : 2 * LANES]
    table[LANES:, :LANES] = jnp.zeros((LANES, LANES), jnp.float32)


def collect(done, kept, received, scale):
    rows, width = kept.shape[0], done.shape[1] + kept.shape[1]
    return pl.pallas_call(
        functools.partial(collect_kernel, scale),
        out_shape=[
            jax.ShapeDtypeStruct((rows, width), jnp.float32),
            jax.ShapeDtypeStruct((rows, width), jnp.float32),
            jax.ShapeDtypeStruct((width + PAD, LANES), jnp.float32),
        ],
        compiler_params=params(),
        name="collect",
    )(done, kept, *received)


def factor(table, r_out):
    width = table.shape[0]
    tiles = width // LANES
    lane = lax.broadcasted_iota(jnp.int32, (SUB, LANES), 1)
    sub = lax.broadcasted_iota(jnp.int32, (SUB, LANES), 0)
    spread = lambda x, k: jnp.broadcast_to(x[k : k + 1], (SUB, LANES))
    groups = BLOCK // SUB
    ahead = table[:BLOCK, :]
    for base in range(0, width, BLOCK):
        t, off = base // LANES, base % LANES
        rows = [
            [ahead[SUB * q : SUB * (q + 1), LANES * i : LANES * (i + 1)] for i in range(tiles)]
            for q in range(groups)
        ]
        for p in range(groups):
            first = off + SUB * p
            cols = [
                [
                    jnp.broadcast_to(rows[q][t][:, first + m : first + m + 1], (SUB, LANES))
                    if q >= p
                    else None
                    for q in range(groups)
                ]
                for m in range(SUB)
            ]
            upper = rows[p][t]
            inside = (lane >= first) & (lane < first + SUB)
            unit = jnp.where(lane - first == sub, 1.0, 0.0)
            for q in range(p, groups):
                rows[q][t] = jnp.where(inside, unit if q == p else 0.0, rows[q][t])
            pivots = jnp.ones((SUB, LANES), jnp.float32)
            for k in range(0, SUB, 2):
                one, two = cols[k], cols[k + 1]
                corner, side, far = spread(one[p], k), spread(two[p], k), spread(two[p], k + 1)
                lead = 1.0 / corner
                whole_ = corner * far - side * side
                both = 1.0 / whole_
                slope = side * lead
                second = jnp.where(sub == k + 1, whole_ * lead, pivots)
                pivots = jnp.where(sub == k, corner, second)
                step, more = [None] * groups, [None] * groups
                for q in range(p, groups):
                    step[q] = (far * one[q] - side * two[q]) * both
                    more[q] = (corner * two[q] - side * one[q]) * both
                step[p] = jnp.where(sub > k + 1, step[p], jnp.where(sub == k + 1, slope, 0.0))
                more[p] = jnp.where(sub > k + 1, more[p], 0.0)
                for m in range(k + 2, SUB):
                    line, next_ = spread(cols[m][p], k), spread(cols[m][p], k + 1)
                    for q in range(p, groups):
                        cols[m][q] = cols[m][q] - step[q] * line - more[q] * next_
                for i in range(tiles):
                    line, next_ = spread(rows[p][i], k), spread(rows[p][i], k + 1)
                    for q in range(p, groups):
                        rows[q][i] = rows[q][i] - step[q] * line - more[q] * next_
                line, next_ = spread(upper, k), spread(upper, k + 1)
                upper = upper - step[p] * line - more[p] * next_
            scale = lax.rsqrt(pivots)
            for i in range(tiles):
                rows[p][i] = rows[p][i] * scale
            upper = jnp.where(lane >= first + SUB, rows[p][t], upper * scale)
            upper = jnp.where(lane >= first + sub, upper, 0.0)
            place = slice(base + SUB * p, base + SUB * (p + 1))
            for i in range(tiles):
                r_out[place, LANES * i : LANES * (i + 1)] = (
                    upper if i == t else rows[p][i] if i > t else jnp.zeros((SUB, LANES), jnp.float32)
                )
        for p in range(groups - 1):
            rows[p][t] = jnp.where((lane >= off + SUB * (p + 1)) & (lane < off + BLOCK), 0.0, rows[p][t])
        whole = jnp.concatenate([jnp.concatenate(r, axis=1) for r in rows], axis=0)
        column = lax.broadcasted_iota(jnp.int32, (BLOCK, width), 1)
        table[base : base + BLOCK, :] = jnp.where(column < base + BLOCK, whole, 0.0)
        end = base + BLOCK
        if end < width:
            h, m, l = pieces(whole)
            left = jnp.concatenate([h, h, h, m, m, l], axis=0).T
            right = jnp.concatenate([h, m, l, h, m, h], axis=0)

            def update(begin, stop):
                change = jnp.dot(left[begin:stop], right, preferred_element_type=jnp.float32)
                column = lax.broadcasted_iota(jnp.int32, (stop - begin, width), 1)
                inside = (column >= base) & (column < end)
                return jnp.where(inside, 0.0, table[begin:stop, :]) - change

            ahead = update(end, end + BLOCK)
            if end + BLOCK < width:
                table[end + BLOCK :, :] = update(end + BLOCK, width)

def basis_kernel(gram, y, r_out, q_out, table):
    unpack_gram(gram, table)
    factor(table, r_out)
    q_out[...] = lax.dot_general(
        y[...],
        table[...],
        (((1,), (1,)), ((), ())),
        precision=HIGH,
        preferred_element_type=jnp.float32,
    )


def orthonormalize(gram, y):
    width = y.shape[1]
    return pl.pallas_call(
        basis_kernel,
        out_shape=[
            jax.ShapeDtypeStruct((width, width), jnp.float32),
            jax.ShapeDtypeStruct(y.shape, jnp.float32),
        ],
        scratch_shapes=[pltpu.VMEM((width, width), jnp.float32)],
        compiler_params=params(),
        name="orthonormalize",
    )(gram, y)


def swap(array, axis, mask):
    size = math.prod(lax.axis_size(name) for name in (axis if isinstance(axis, tuple) else (axis,)))
    return lax.ppermute(array, axis, [(i, i ^ mask) for i in range(size)])


def both(mine, got, first):
    return jnp.concatenate([jnp.where(first, mine, got), jnp.where(first, got, mine)], axis=0)


def gram_total(gram):
    rows, width = gram.shape
    if lax.axis_size("snp") != 4 or lax.axis_size("samp") != 4:
        return lax.psum(gram, ("samp", "snp"))
    bit = jnp.bitwise_and(lax.axis_index("snp"), 1)
    halves = gram.reshape(2, rows // 2, width)
    mine, other = (lax.dynamic_index_in_dim(halves, b, 0, keepdims=False) for b in (bit, 1 - bit))
    part = mine + swap(other, "snp", 1)
    part = part + swap(part, "snp", 2)
    part = (part + swap(part, "samp", 1)) + (swap(part, "samp", 2) + swap(part, "samp", 3))
    return both(part, swap(part, "snp", 1), bit == 0)


def per_device(genotypes, basis_cols):
    n_snp, n_samp = lax.axis_size("snp"), lax.axis_size("samp")
    bits = n_snp.bit_length() - 1
    words, snps = genotypes.shape
    width = basis_cols.shape[1]
    samples = words * PLANES * n_samp
    inv_root = float(1.0 / samples**0.5)
    chunk = snps // n_samp
    direct = n_samp <= 4 and chunk % LANES == 0

    other, sums = project(genotypes, basis_cols, True)
    got = swap(other, "snp", 1)
    if n_snp <= 4:
        more = sum(swap(sums, "snp", mask) for mask in range(1, n_snp))
    else:
        more = lax.psum(sums, "snp") - sums
    (mine,) = project(genotypes, basis_cols, False)
    *parts, sums = merge(mine, got, sums, more, 2)
    if n_samp <= 4:
        for b in range(n_samp.bit_length() - 1):
            sums = sums + swap(sums, "samp", 1 << b)
    else:
        sums = lax.psum(sums, "samp")

    kept, received = [], []
    got, sent = None, None
    for group, part in enumerate(parts):
        if got is not None:
            part, _, _ = lax.optimization_barrier((part, got, sums))
        for b in range(1, bits - 1):
            part = part + swap(part, "snp", 1 << b)
        got = swap(part, "snp", 1 << (bits - 1))
        ready = got
        if sent is not None:
            ready, _ = lax.optimization_barrier((got, sent))
        rows = finish(part, ready, sums, samples, group)
        scores = (rows, swap(rows, "snp", 1))
        if direct:
            masks = (2, 1, 3)
            coded = list(chunks_of_y(genotypes, scores, chunk, inv_root, masks[:1]))
            *others, own = chunks_of_y(genotypes, scores, chunk, inv_root, masks[1:] + (0,))
            coded += others
            kept.append(own)
            received.append([swap(c, "samp", mask) for c, mask in zip(coded, masks)])
            sent = (received[-1][0], own)
        else:
            tile = 4 * LANES if snps % (4 * LANES) == 0 else snps
            tiles = [
                chunks_of_y(genotypes, scores, tile, inv_root, piece=i)[0]
                for i in range(snps // tile)
            ]
            whole = jnp.concatenate(tiles, axis=0)
            kept.append(lax.psum_scatter(whole, "samp", scatter_dimension=0, tiled=True))
            received.append([])
    done = add_chunks(kept[0], received[0]) if direct else kept[0]
    y_local, y_again, gram = collect(done, kept[1], received[1], 1.0 / (snps * n_snp))
    gram_sum = gram_total(gram)
    r_factor, q_next = orthonormalize(gram_sum, y_again)
    layout = (1, 1, y_local.shape[0], width)
    return (y_local.reshape(layout), r_factor, q_next.reshape(layout))


def solution(mesh):
    return jax.shard_map(
        per_device,
        mesh=mesh,
        in_specs=(P(("grp", "samp"), "snp"), P(("grp", "snp"), None)),
        out_specs=(
            P(("grp", "snp"), "samp", None, None),
            P("grp", None),
            P(("grp", "snp"), "samp", None, None),
        ),
        check_vma=False,
    )
```

```python
import functools
import math

import jax
import jax.numpy as jnp
from jax import lax
from jax.experimental import pallas as pl
from jax.experimental.pallas import tpu as pltpu
from jax.sharding import PartitionSpec as P

PLANES = 6
STEPS = 64.0
TOP = 32767.0
BLOCK, LANES, SUB, PAD = 32, 128, 8, 32
HIGH = lax.Precision.HIGHEST
PAIRS = 0x333
VMEM_BYTES = 40 * 1024 * 1024


def params(**more):
    return pltpu.CompilerParams(vmem_limit_bytes=VMEM_BYTES, **more)


def planes_of(words):
    return [
        jnp.bitwise_and(jnp.right_shift(words, 2 * t), 3).astype(jnp.float32).astype(jnp.bfloat16)
        for t in range(PLANES)
    ]


def half_rows(words, basis, out, place):
    half = words.shape[0] // 2
    part = words[pl.ds(pl.multiple_of(place * half, half), half)]
    for t, plane in enumerate(planes_of(part)):
        out[t] = jnp.dot(plane, basis[...], preferred_element_type=jnp.float32)


def low_bit():
    return jnp.bitwise_and(lax.axis_index("snp"), 1)


def counts_of(words):
    total = None
    groups = words.shape[0] // 8
    for first in range(0, groups, 3):
        held = None
        for g in range(first, min(first + 3, groups)):
            word = words[8 * g : 8 * g + 8]
            pair = (word & PAIRS) + (jnp.right_shift(word, 2) & PAIRS)
            held = pair if held is None else held + pair
        held = (held & 15) + (jnp.right_shift(held, 4) & 15) + jnp.right_shift(held, 8)
        total = held if total is None else total + held
    return total


def other_kernel(words, basis, out, sums):
    counts = counts_of(words)
    pieces_ = jnp.concatenate([jnp.right_shift(counts, 4), counts & 15], axis=0)
    both_ = jnp.dot(
        pieces_.astype(jnp.float32).astype(jnp.bfloat16),
        basis[...],
        preferred_element_type=jnp.float32,
    )
    sums[...] = 16.0 * both_[:8] + both_[8:]
    half_rows(words, basis, out, 1 - low_bit())


def mine_kernel(words, basis, out):
    half_rows(words, basis, out, low_bit())


def project(words, basis, other):
    count, snps = words.shape
    width = basis.shape[1]
    half = count // 2
    shapes = [jax.ShapeDtypeStruct((PLANES, half, width), jnp.float32)]
    if other:
        shapes.append(jax.ShapeDtypeStruct((8, width), jnp.float32))
    return pl.pallas_call(
        other_kernel if other else mine_kernel,
        out_shape=shapes,
        compiler_params=params(),
        name="project_other" if other else "project_mine",
        cost_estimate=pl.CostEstimate(
            flops=2 * half * PLANES * snps * width,
            bytes_accessed=4 * half * snps + 2 * snps * width + 4 * half * PLANES * width,
            transcendentals=0,
        ),
    )(words, basis)


def merge_kernel(mine, got, sums, more, *outs):
    span = outs[0].shape[-1]
    for i, out in enumerate(outs[:-1]):
        columns = slice(i * span, (i + 1) * span)
        out[...] = mine[:, :, columns] + got[:, :, columns]
    outs[-1][...] = sums[...] + more[...]


def merge(mine, got, sums, more, groups):
    shape = mine.shape[:2] + (mine.shape[2] // groups,)
    return pl.pallas_call(
        merge_kernel,
        out_shape=[jax.ShapeDtypeStruct(shape, jnp.float32)] * groups
        + [jax.ShapeDtypeStruct(sums.shape, jnp.float32)],
        compiler_params=params(),
        name="merge",
    )(mine, got, sums, more)


def finish_kernel(samples, group, mine, got, sums, out):
    span = out.shape[-1]
    columns = sums[:, group * span : (group + 1) * span]
    center = jnp.sum(columns, axis=0, keepdims=True) / jnp.float32(samples)
    out[...] = (mine[...] + got[...] - center[None]).astype(jnp.bfloat16)


def finish(mine, got, sums, samples, group):
    return pl.pallas_call(
        functools.partial(finish_kernel, samples, group),
        out_shape=jax.ShapeDtypeStruct(mine.shape, jnp.bfloat16),
        compiler_params=params(),
        name="finish",
    )(mine, got, sums)


def back_project(words, mine, other, scale):
    total = None
    for t, plane in enumerate(planes_of(words)):
        rows = jnp.concatenate([mine[t], other[t]], axis=0)
        term = lax.dot_general(
            rows, plane, (((0,), (0,)), ((), ())), preferred_element_type=jnp.float32
        )
        total = term if total is None else total + term
    return (total * scale).T


def chunk_value(scale, mask, piece, words, mine, other, rows):
    index = piece if mask is None else jnp.bitwise_xor(lax.axis_index("samp"), mask)
    span = pl.ds(pl.multiple_of(index * rows, rows), rows)
    half = words.shape[0] // 2
    first, second = (
        words[pl.ds(pl.multiple_of(place * half, half), half), span]
        for place in (low_bit(), 1 - low_bit())
    )
    return back_project(jnp.concatenate([first, second], axis=0), mine, other, scale)


def encode(value, out):
    rows = value.shape[0]
    top = jnp.maximum(jnp.max(jnp.abs(value), axis=0, keepdims=True), 1e-30)
    level = jnp.ceil(STEPS * jnp.log2(top / TOP)) + 1.0
    unit = jnp.exp2(level * (1.0 / STEPS))
    coded = jnp.clip(jnp.round(value * (1.0 / unit)), -TOP, TOP)
    out[:rows] = coded.astype(jnp.int32).astype(jnp.int16)
    out[rows:] = jnp.broadcast_to(level, (16, level.shape[1])).astype(jnp.int32).astype(jnp.int16)


def chunks_kernel(scale, masks, rows, words, mine, other, *outs):
    for mask, out in zip(masks, outs):
        value = chunk_value(scale, mask, 0, words, mine, other, rows)
        if mask:
            encode(value, out)
        else:
            out[...] = value


def piece_kernel(scale, piece, words, mine, other, out):
    out[...] = chunk_value(scale, None, piece, words, mine, other, out.shape[0])


def chunks_of_y(words, scores, rows, scale, masks=None, piece=None):
    width = scores[0].shape[-1]
    if masks is None:
        kernel = functools.partial(piece_kernel, scale, piece)
        shapes = [jax.ShapeDtypeStruct((rows, width), jnp.float32)]
    else:
        kernel = functools.partial(chunks_kernel, scale, masks, rows)
        shapes = [
            jax.ShapeDtypeStruct((rows + 16, width), jnp.int16)
            if mask
            else jax.ShapeDtypeStruct((rows, width), jnp.float32)
            for mask in masks
        ]
    return pl.pallas_call(
        kernel,
        out_shape=shapes,
        compiler_params=params(),
        name="chunks",
        cost_estimate=pl.CostEstimate(
            flops=2 * words.shape[0] * PLANES * rows * width * len(shapes),
            bytes_accessed=(4 * words.shape[0] + 4 * width) * rows * len(shapes),
            transcendentals=0,
        ),
    )(words, *scores)


def decoded(coded, rows):
    level = coded[rows : rows + 16].astype(jnp.int32).astype(jnp.float32)[:1]
    return coded[:rows].astype(jnp.int32).astype(jnp.float32) * jnp.exp2(level * (1.0 / STEPS))


def add_kernel(kept, *refs):
    total = kept[...]
    for ref in refs[:-1]:
        total = total + decoded(ref, kept.shape[0])
    refs[-1][...] = total


def add_chunks(kept, received):
    return pl.pallas_call(
        add_kernel,
        out_shape=jax.ShapeDtypeStruct(kept.shape, jnp.float32),
        compiler_params=params(),
        name="add_chunks",
        cost_estimate=pl.CostEstimate(
            flops=4 * kept.size, bytes_accessed=10 * kept.size, transcendentals=0
        ),
    )(kept, *received)


def pieces(x):
    high = x.astype(jnp.bfloat16)
    rest = x - high.astype(jnp.float32)
    mid = rest.astype(jnp.bfloat16)
    low = (rest - mid.astype(jnp.float32)).astype(jnp.bfloat16)
    return high, mid, low

def gram_blocks(total):
    high, mid, low = pieces(total)
    rows = (((0,), (0,)), ((), ()))
    product = functools.partial(
        lax.dot_general, dimension_numbers=rows, preferred_element_type=jnp.float32
    )
    small = product(high, mid) + product(high, low)
    whole = product(high, high) + (product(mid, mid) + (small + small.T))
    return whole[:LANES, :LANES], whole[:LANES, LANES:], whole[LANES:, LANES:]


def collect_kernel(scale, done, kept, *refs):
    out, copy, gram = refs[-3:]
    last = kept[...]
    for ref in refs[:-3]:
        last = last + decoded(ref, kept.shape[0])
    total = jnp.concatenate([done[...], last], axis=1)
    out[...] = total
    copy[...] = total
    first, corner, second = (scale * block for block in gram_blocks(total))

    row = lax.broadcasted_iota(jnp.int32, first.shape, 0)
    column = lax.broadcasted_iota(jnp.int32, first.shape, 1)
    gram[:LANES] = jnp.where(row <= column, first, second)
    gram[LANES : 2 * LANES] = corner
    gram[2 * LANES :] = jnp.zeros((PAD, LANES), jnp.float32)
    gram[2 * LANES : 2 * LANES + 1] = jnp.sum(
        jnp.where(row == column, second, 0.0), axis=0, keepdims=True
    )


def unpack_gram(packed, table):
    mixed = packed[:LANES]
    turned = mixed.T
    row = lax.broadcasted_iota(jnp.int32, mixed.shape, 0)
    column = lax.broadcasted_iota(jnp.int32, mixed.shape, 1)
    table[:LANES, :LANES] = jnp.where(row <= column, mixed, turned)
    second = jnp.where(row > column, mixed, turned)
    table[LANES:, LANES:] = jnp.where(row == column, packed[2 * LANES : 2 * LANES + 1], second)
    table[:LANES, LANES:] = packed[LANES : 2 * LANES]
    table[LANES:, :LANES] = jnp.zeros((LANES, LANES), jnp.float32)


def collect(done, kept, received, scale):
    rows, width = kept.shape[0], done.shape[1] + kept.shape[1]
    return pl.pallas_call(
        functools.partial(collect_kernel, scale),
        out_shape=[
            jax.ShapeDtypeStruct((rows, width), jnp.float32),
            jax.ShapeDtypeStruct((rows, width), jnp.float32),
            jax.ShapeDtypeStruct((width + PAD, LANES), jnp.float32),
        ],
        compiler_params=params(),
        name="collect",
    )(done, kept, *received)


def factor(table, r_out):
    width = table.shape[0]
    tiles = width // LANES
    lane = lax.broadcasted_iota(jnp.int32, (SUB, LANES), 1)
    sub = lax.broadcasted_iota(jnp.int32, (SUB, LANES), 0)
    spread = lambda x, k: jnp.broadcast_to(x[k : k + 1], (SUB, LANES))
    groups = BLOCK // SUB
    ahead = table[:BLOCK, :]
    for base in range(0, width, BLOCK):
        t, off = base // LANES, base % LANES
        rows = [
            [ahead[SUB * q : SUB * (q + 1), LANES * i : LANES * (i + 1)] for i in range(tiles)]
            for q in range(groups)
        ]
        for p in range(groups):
            first = off + SUB * p
            cols = [
                [
                    jnp.broadcast_to(rows[q][t][:, first + m : first + m + 1], (SUB, LANES))
                    if q >= p
                    else None
                    for q in range(groups)
                ]
                for m in range(SUB)
            ]
            upper = rows[p][t]
            inside = (lane >= first) & (lane < first + SUB)
            unit = jnp.where(lane - first == sub, 1.0, 0.0)
            for q in range(p, groups):
                rows[q][t] = jnp.where(inside, unit if q == p else 0.0, rows[q][t])
            pivots = jnp.ones((SUB, LANES), jnp.float32)
            for k in range(0, SUB, 2):
                one, two = cols[k], cols[k + 1]
                corner, side, far = spread(one[p], k), spread(two[p], k), spread(two[p], k + 1)
                lead = 1.0 / corner
                whole_ = corner * far - side * side
                both = 1.0 / whole_
                slope = side * lead
                second = jnp.where(sub == k + 1, whole_ * lead, pivots)
                pivots = jnp.where(sub == k, corner, second)
                step, more = [None] * groups, [None] * groups
                for q in range(p, groups):
                    step[q] = (far * one[q] - side * two[q]) * both
                    more[q] = (corner * two[q] - side * one[q]) * both
                step[p] = jnp.where(sub > k + 1, step[p], jnp.where(sub == k + 1, slope, 0.0))
                more[p] = jnp.where(sub > k + 1, more[p], 0.0)
                for m in range(k + 2, SUB):
                    line, next_ = spread(cols[m][p], k), spread(cols[m][p], k + 1)
                    for q in range(p, groups):
                        cols[m][q] = cols[m][q] - step[q] * line - more[q] * next_
                for i in range(tiles):
                    line, next_ = spread(rows[p][i], k), spread(rows[p][i], k + 1)
                    for q in range(p, groups):
                        rows[q][i] = rows[q][i] - step[q] * line - more[q] * next_
                line, next_ = spread(upper, k), spread(upper, k + 1)
                upper = upper - step[p] * line - more[p] * next_
            scale = lax.rsqrt(pivots)
            for i in range(tiles):
                rows[p][i] = rows[p][i] * scale
            upper = jnp.where(lane >= first + SUB, rows[p][t], upper * scale)
            upper = jnp.where(lane >= first + sub, upper, 0.0)
            place = slice(base + SUB * p, base + SUB * (p + 1))
            for i in range(tiles):
                r_out[place, LANES * i : LANES * (i + 1)] = (
                    upper if i == t else rows[p][i] if i > t else jnp.zeros((SUB, LANES), jnp.float32)
                )
        for p in range(groups - 1):
            rows[p][t] = jnp.where((lane >= off + SUB * (p + 1)) & (lane < off + BLOCK), 0.0, rows[p][t])
        whole = jnp.concatenate([jnp.concatenate(r, axis=1) for r in rows], axis=0)
        column = lax.broadcasted_iota(jnp.int32, (BLOCK, width), 1)
        table[base : base + BLOCK, :] = jnp.where(column < base + BLOCK, whole, 0.0)
        end = base + BLOCK
        if end < width:
            h, m, l = pieces(whole)
            left = jnp.concatenate([h, h, h, m, m, l], axis=0).T
            right = jnp.concatenate([h, m, l, h, m, h], axis=0)

            def update(begin, stop):
                change = jnp.dot(left[begin:stop], right, preferred_element_type=jnp.float32)
                column = lax.broadcasted_iota(jnp.int32, (stop - begin, width), 1)
                inside = (column >= base) & (column < end)
                return jnp.where(inside, 0.0, table[begin:stop, :]) - change

            ahead = update(end, end + BLOCK)
            if end + BLOCK < width:
                table[end + BLOCK :, :] = update(end + BLOCK, width)

def basis_kernel(gram, y, r_out, q_out, table):
    unpack_gram(gram, table)
    factor(table, r_out)
    q_out[...] = lax.dot_general(
        y[...],
        table[...],
        (((1,), (1,)), ((), ())),
        precision=HIGH,
        preferred_element_type=jnp.float32,
    )


def orthonormalize(gram, y):
    width = y.shape[1]
    return pl.pallas_call(
        basis_kernel,
        out_shape=[
            jax.ShapeDtypeStruct((width, width), jnp.float32),
            jax.ShapeDtypeStruct(y.shape, jnp.float32),
        ],
        scratch_shapes=[pltpu.VMEM((width, width), jnp.float32)],
        compiler_params=params(),
        name="orthonormalize",
    )(gram, y)


def swap(array, axis, mask):
    size = math.prod(lax.axis_size(name) for name in (axis if isinstance(axis, tuple) else (axis,)))
    return lax.ppermute(array, axis, [(i, i ^ mask) for i in range(size)])


def both(mine, got, first):
    return jnp.concatenate([jnp.where(first, mine, got), jnp.where(first, got, mine)], axis=0)


def gram_total(gram):
    rows, width = gram.shape
    if lax.axis_size("snp") != 4 or lax.axis_size("samp") != 4:
        return lax.psum(gram, ("samp", "snp"))
    bit = jnp.bitwise_and(lax.axis_index("snp"), 1)
    halves = gram.reshape(2, rows // 2, width)
    mine, other = (lax.dynamic_index_in_dim(halves, b, 0, keepdims=False) for b in (bit, 1 - bit))
    part = mine + swap(other, "snp", 1)
    part = part + swap(part, "snp", 2)
    part = part + swap(part, "samp", 1)
    part = part + swap(part, "samp", 2)
    return both(part, swap(part, "snp", 1), bit == 0)


def per_device(genotypes, basis_cols):
    n_snp, n_samp = lax.axis_size("snp"), lax.axis_size("samp")
    bits = n_snp.bit_length() - 1
    words, snps = genotypes.shape
    width = basis_cols.shape[1]
    samples = words * PLANES * n_samp
    inv_root = float(1.0 / samples**0.5)
    chunk = snps // n_samp
    direct = n_samp in (2, 4) and chunk % LANES == 0

    other, sums = project(genotypes, basis_cols, True)
    got = swap(other, "snp", 1)
    more = swap(sums, "snp", 1 << (bits - 1))
    (mine,) = project(genotypes, basis_cols, False)
    *parts, sums = merge(mine, got, sums, more, 2)
    for b in range(bits - 1):
        sums = sums + swap(sums, "snp", 1 << b)
    if n_samp <= 4:
        for b in range(n_samp.bit_length() - 1):
            sums = sums + swap(sums, "samp", 1 << b)
    else:
        sums = lax.psum(sums, "samp")

    kept, received = [], []
    got, sent = None, None
    for group, part in enumerate(parts):
        if got is not None:
            part, _, _ = lax.optimization_barrier((part, got, sums))
        for b in range(1, bits - 1):
            part = part + swap(part, "snp", 1 << b)
        got = swap(part, "snp", 1 << (bits - 1))
        ready = got
        if sent is not None:
            ready, _ = lax.optimization_barrier((got, sent))
        rows = finish(part, ready, sums, samples, group)
        scores = (rows, swap(rows, "snp", 1))
        if direct:
            masks = (2, 3, 1) if n_samp == 4 else (1,)
            coded = list(chunks_of_y(genotypes, scores, chunk, inv_root, masks[:1]))
            *others, own = chunks_of_y(genotypes, scores, chunk, inv_root, masks[1:] + (0,))
            coded += others
            kept.append(own)
            received.append([swap(c, "samp", mask) for c, mask in zip(coded, masks)])
            sent = (received[-1][0], own)
        else:
            tile = 4 * LANES if snps % (4 * LANES) == 0 else snps
            tiles = [
                chunks_of_y(genotypes, scores, tile, inv_root, piece=i)[0]
                for i in range(snps // tile)
            ]
            whole = jnp.concatenate(tiles, axis=0)
            kept.append(lax.psum_scatter(whole, "samp", scatter_dimension=0, tiled=True))
            received.append([])
    done = add_chunks(kept[0], received[0]) if direct else kept[0]
    y_local, y_again, gram = collect(done, kept[1], received[1], 1.0 / (snps * n_snp))
    gram_sum = gram_total(gram)
    r_factor, q_next = orthonormalize(gram_sum, y_again)
    layout = (1, 1, y_local.shape[0], width)
    return (y_local.reshape(layout), r_factor, q_next.reshape(layout))


def solution(mesh):
    return jax.shard_map(
        per_device,
        mesh=mesh,
        in_specs=(P(("grp", "samp"), "snp"), P(("grp", "snp"), None)),
        out_specs=(
            P(("grp", "snp"), "samp", None, None),
            P("grp", None),
            P(("grp", "snp"), "samp", None, None),
        ),
        check_vma=False,
    )
```

```python
import functools
import math

import jax
import jax.numpy as jnp
from jax import lax
from jax.experimental import pallas as pl
from jax.experimental.pallas import tpu as pltpu
from jax.sharding import PartitionSpec as P

PLANES = 6
STEPS = 64.0
TOP = 32767.0
BLOCK, LANES, SUB, PAD = 32, 128, 8, 32
HIGH = lax.Precision.HIGHEST
PAIRS = 0x333
VMEM_BYTES = 40 * 1024 * 1024


def params(**more):
    return pltpu.CompilerParams(vmem_limit_bytes=VMEM_BYTES, **more)


def planes_of(words):
    return [
        jnp.bitwise_and(jnp.right_shift(words, 2 * t), 3).astype(jnp.float32).astype(jnp.bfloat16)
        for t in range(PLANES)
    ]


def half_rows(words, basis, out, place):
    half = words.shape[0] // 2
    part = words[pl.ds(pl.multiple_of(place * half, half), half)]
    for t, plane in enumerate(planes_of(part)):
        out[t] = jnp.dot(plane, basis[...], preferred_element_type=jnp.float32)


def low_bit():
    return jnp.bitwise_and(lax.axis_index("snp"), 1)


def counts_of(words):
    total = None
    groups = words.shape[0] // 8
    for first in range(0, groups, 3):
        held = None
        for g in range(first, min(first + 3, groups)):
            word = words[8 * g : 8 * g + 8]
            pair = (word & PAIRS) + (jnp.right_shift(word, 2) & PAIRS)
            held = pair if held is None else held + pair
        held = (held & 15) + (jnp.right_shift(held, 4) & 15) + jnp.right_shift(held, 8)
        total = held if total is None else total + held
    return total


def other_kernel(words, basis, out, sums):
    counts = counts_of(words)
    pieces_ = jnp.concatenate([jnp.right_shift(counts, 4), counts & 15], axis=0)
    both_ = jnp.dot(
        pieces_.astype(jnp.float32).astype(jnp.bfloat16),
        basis[...],
        preferred_element_type=jnp.float32,
    )
    sums[...] = 16.0 * both_[:8] + both_[8:]
    half_rows(words, basis, out, 1 - low_bit())


def mine_kernel(words, basis, out):
    half_rows(words, basis, out, low_bit())


def project(words, basis, other):
    count, snps = words.shape
    width = basis.shape[1]
    half = count // 2
    shapes = [jax.ShapeDtypeStruct((PLANES, half, width), jnp.float32)]
    if other:
        shapes.append(jax.ShapeDtypeStruct((8, width), jnp.float32))
    return pl.pallas_call(
        other_kernel if other else mine_kernel,
        out_shape=shapes,
        compiler_params=params(),
        name="project_other" if other else "project_mine",
        cost_estimate=pl.CostEstimate(
            flops=2 * half * PLANES * snps * width,
            bytes_accessed=4 * half * snps + 2 * snps * width + 4 * half * PLANES * width,
            transcendentals=0,
        ),
    )(words, basis)


def merge_kernel(mine, got, sums, more, *outs):
    span = outs[0].shape[-1]
    for i, out in enumerate(outs[:-1]):
        columns = slice(i * span, (i + 1) * span)
        out[...] = mine[:, :, columns] + got[:, :, columns]
    outs[-1][...] = sums[...] + more[...]


def merge(mine, got, sums, more, groups):
    shape = mine.shape[:2] + (mine.shape[2] // groups,)
    return pl.pallas_call(
        merge_kernel,
        out_shape=[jax.ShapeDtypeStruct(shape, jnp.float32)] * groups
        + [jax.ShapeDtypeStruct(sums.shape, jnp.float32)],
        compiler_params=params(),
        name="merge",
    )(mine, got, sums, more)


def finish_kernel(samples, group, mine, got, sums, out):
    span = out.shape[-1]
    columns = sums[:, group * span : (group + 1) * span]
    center = jnp.sum(columns, axis=0, keepdims=True) / jnp.float32(samples)
    out[...] = (mine[...] + got[...] - center[None]).astype(jnp.bfloat16)


def finish(mine, got, sums, samples, group):
    return pl.pallas_call(
        functools.partial(finish_kernel, samples, group),
        out_shape=jax.ShapeDtypeStruct(mine.shape, jnp.bfloat16),
        compiler_params=params(),
        name="finish",
    )(mine, got, sums)


def back_project(words, mine, other, scale):
    total = None
    for t, plane in enumerate(planes_of(words)):
        rows = jnp.concatenate([mine[t], other[t]], axis=0)
        term = lax.dot_general(
            rows, plane, (((0,), (0,)), ((), ())), preferred_element_type=jnp.float32
        )
        total = term if total is None else total + term
    return (total * scale).T


def chunk_value(scale, mask, piece, words, mine, other, rows):
    index = piece if mask is None else jnp.bitwise_xor(lax.axis_index("samp"), mask)
    span = pl.ds(pl.multiple_of(index * rows, rows), rows)
    half = words.shape[0] // 2
    first, second = (
        words[pl.ds(pl.multiple_of(place * half, half), half), span]
        for place in (low_bit(), 1 - low_bit())
    )
    return back_project(jnp.concatenate([first, second], axis=0), mine, other, scale)


def encode(value, out):
    rows = value.shape[0]
    top = jnp.maximum(jnp.max(jnp.abs(value), axis=0, keepdims=True), 1e-30)
    level = jnp.ceil(STEPS * jnp.log2(top / TOP)) + 1.0
    unit = jnp.exp2(level * (1.0 / STEPS))
    coded = jnp.clip(jnp.round(value * (1.0 / unit)), -TOP, TOP)
    out[:rows] = coded.astype(jnp.int32).astype(jnp.int16)
    out[rows:] = jnp.broadcast_to(level, (16, level.shape[1])).astype(jnp.int32).astype(jnp.int16)


def chunks_kernel(scale, masks, rows, words, mine, other, *outs):
    for mask, out in zip(masks, outs):
        value = chunk_value(scale, mask, 0, words, mine, other, rows)
        if mask:
            encode(value, out)
        else:
            out[...] = value


def piece_kernel(scale, piece, words, mine, other, out):
    out[...] = chunk_value(scale, None, piece, words, mine, other, out.shape[0])


def chunks_of_y(words, scores, rows, scale, masks=None, piece=None):
    width = scores[0].shape[-1]
    if masks is None:
        kernel = functools.partial(piece_kernel, scale, piece)
        shapes = [jax.ShapeDtypeStruct((rows, width), jnp.float32)]
    else:
        kernel = functools.partial(chunks_kernel, scale, masks, rows)
        shapes = [
            jax.ShapeDtypeStruct((rows + 16, width), jnp.int16)
            if mask
            else jax.ShapeDtypeStruct((rows, width), jnp.float32)
            for mask in masks
        ]
    return pl.pallas_call(
        kernel,
        out_shape=shapes,
        compiler_params=params(),
        name="chunks",
        cost_estimate=pl.CostEstimate(
            flops=2 * words.shape[0] * PLANES * rows * width * len(shapes),
            bytes_accessed=(4 * words.shape[0] + 4 * width) * rows * len(shapes),
            transcendentals=0,
        ),
    )(words, *scores)


def decoded(coded, rows):
    level = coded[rows : rows + 16].astype(jnp.int32).astype(jnp.float32)[:1]
    return coded[:rows].astype(jnp.int32).astype(jnp.float32) * jnp.exp2(level * (1.0 / STEPS))


def add_kernel(kept, *refs):
    total = kept[...]
    for ref in refs[:-1]:
        total = total + decoded(ref, kept.shape[0])
    refs[-1][...] = total


def add_chunks(kept, received):
    return pl.pallas_call(
        add_kernel,
        out_shape=jax.ShapeDtypeStruct(kept.shape, jnp.float32),
        compiler_params=params(),
        name="add_chunks",
        cost_estimate=pl.CostEstimate(
            flops=4 * kept.size, bytes_accessed=10 * kept.size, transcendentals=0
        ),
    )(kept, *received)


def pieces(x):
    high = x.astype(jnp.bfloat16)
    rest = x - high.astype(jnp.float32)
    mid = rest.astype(jnp.bfloat16)
    low = (rest - mid.astype(jnp.float32)).astype(jnp.bfloat16)
    return high, mid, low

def gram_blocks(total):
    high, mid, low = pieces(total)
    rows = (((0,), (0,)), ((), ()))
    product = functools.partial(
        lax.dot_general, dimension_numbers=rows, preferred_element_type=jnp.float32
    )
    small = product(high, mid) + product(high, low)
    whole = product(high, high) + (product(mid, mid) + (small + small.T))
    return whole[:LANES, :LANES], whole[:LANES, LANES:], whole[LANES:, LANES:]


def collect_kernel(scale, done, kept, *refs):
    out, copy, gram = refs[-3:]
    last = kept[...]
    for ref in refs[:-3]:
        last = last + decoded(ref, kept.shape[0])
    total = jnp.concatenate([done[...], last], axis=1)
    out[...] = total
    copy[...] = total
    first, corner, second = (scale * block for block in gram_blocks(total))

    row = lax.broadcasted_iota(jnp.int32, first.shape, 0)
    column = lax.broadcasted_iota(jnp.int32, first.shape, 1)
    gram[:LANES] = jnp.where(row <= column, first, second)
    gram[LANES : 2 * LANES] = corner
    gram[2 * LANES :] = jnp.zeros((PAD, LANES), jnp.float32)
    gram[2 * LANES : 2 * LANES + 1] = jnp.sum(
        jnp.where(row == column, second, 0.0), axis=0, keepdims=True
    )


def unpack_gram(packed, table):
    mixed = packed[:LANES]
    turned = mixed.T
    row = lax.broadcasted_iota(jnp.int32, mixed.shape, 0)
    column = lax.broadcasted_iota(jnp.int32, mixed.shape, 1)
    table[:LANES, :LANES] = jnp.where(row <= column, mixed, turned)
    second = jnp.where(row > column, mixed, turned)
    table[LANES:, LANES:] = jnp.where(row == column, packed[2 * LANES : 2 * LANES + 1], second)
    table[:LANES, LANES:] = packed[LANES : 2 * LANES]
    table[LANES:, :LANES] = jnp.zeros((LANES, LANES), jnp.float32)


def collect(done, kept, received, scale):
    rows, width = kept.shape[0], done.shape[1] + kept.shape[1]
    return pl.pallas_call(
        functools.partial(collect_kernel, scale),
        out_shape=[
            jax.ShapeDtypeStruct((rows, width), jnp.float32),
            jax.ShapeDtypeStruct((rows, width), jnp.float32),
            jax.ShapeDtypeStruct((width + PAD, LANES), jnp.float32),
        ],
        compiler_params=params(),
        name="collect",
    )(done, kept, *received)


def factor(table, r_out):
    width = table.shape[0]
    tiles = width // LANES
    lane = lax.broadcasted_iota(jnp.int32, (SUB, LANES), 1)
    sub = lax.broadcasted_iota(jnp.int32, (SUB, LANES), 0)
    spread = lambda x, k: jnp.broadcast_to(x[k : k + 1], (SUB, LANES))
    groups = BLOCK // SUB
    ahead = table[:BLOCK, :]
    for base in range(0, width, BLOCK):
        t, off = base // LANES, base % LANES
        rows = [
            [ahead[SUB * q : SUB * (q + 1), LANES * i : LANES * (i + 1)] for i in range(tiles)]
            for q in range(groups)
        ]
        for p in range(groups):
            first = off + SUB * p
            cols = [
                [
                    jnp.broadcast_to(rows[q][t][:, first + m : first + m + 1], (SUB, LANES))
                    if q >= p
                    else None
                    for q in range(groups)
                ]
                for m in range(SUB)
            ]
            upper = rows[p][t]
            inside = (lane >= first) & (lane < first + SUB)
            unit = jnp.where(lane - first == sub, 1.0, 0.0)
            for q in range(p, groups):
                rows[q][t] = jnp.where(inside, unit if q == p else 0.0, rows[q][t])
            pivots = jnp.ones((SUB, LANES), jnp.float32)
            for k in range(0, SUB, 2):
                one, two = cols[k], cols[k + 1]
                corner, side, far = spread(one[p], k), spread(two[p], k), spread(two[p], k + 1)
                lead = 1.0 / corner
                whole_ = corner * far - side * side
                both = 1.0 / whole_
                slope = side * lead
                second = jnp.where(sub == k + 1, whole_ * lead, pivots)
                pivots = jnp.where(sub == k, corner, second)
                step, more = [None] * groups, [None] * groups
                for q in range(p, groups):
                    step[q] = (far * one[q] - side * two[q]) * both
                    more[q] = (corner * two[q] - side * one[q]) * both
                step[p] = jnp.where(sub > k + 1, step[p], jnp.where(sub == k + 1, slope, 0.0))
                more[p] = jnp.where(sub > k + 1, more[p], 0.0)
                for m in range(k + 2, SUB):
                    line, next_ = spread(cols[m][p], k), spread(cols[m][p], k + 1)
                    for q in range(p, groups):
                        cols[m][q] = cols[m][q] - step[q] * line - more[q] * next_
                for i in range(tiles):
                    line, next_ = spread(rows[p][i], k), spread(rows[p][i], k + 1)
                    for q in range(p, groups):
                        rows[q][i] = rows[q][i] - step[q] * line - more[q] * next_
                line, next_ = spread(upper, k), spread(upper, k + 1)
                upper = upper - step[p] * line - more[p] * next_
            scale = lax.rsqrt(pivots)
            for i in range(tiles):
                rows[p][i] = rows[p][i] * scale
            upper = jnp.where(lane >= first + SUB, rows[p][t], upper * scale)
            upper = jnp.where(lane >= first + sub, upper, 0.0)
            place = slice(base + SUB * p, base + SUB * (p + 1))
            for i in range(tiles):
                r_out[place, LANES * i : LANES * (i + 1)] = (
                    upper if i == t else rows[p][i] if i > t else jnp.zeros((SUB, LANES), jnp.float32)
                )
        for p in range(groups - 1):
            rows[p][t] = jnp.where((lane >= off + SUB * (p + 1)) & (lane < off + BLOCK), 0.0, rows[p][t])
        whole = jnp.concatenate([jnp.concatenate(r, axis=1) for r in rows], axis=0)
        column = lax.broadcasted_iota(jnp.int32, (BLOCK, width), 1)
        table[base : base + BLOCK, :] = jnp.where(column < base + BLOCK, whole, 0.0)
        end = base + BLOCK
        if end < width:
            h, m, l = pieces(whole)
            left = jnp.concatenate([h, h, h, m, m, l], axis=0).T
            right = jnp.concatenate([h, m, l, h, m, h], axis=0)

            def update(begin, stop):
                change = jnp.dot(left[begin:stop], right, preferred_element_type=jnp.float32)
                column = lax.broadcasted_iota(jnp.int32, (stop - begin, width), 1)
                inside = (column >= base) & (column < end)
                return jnp.where(inside, 0.0, table[begin:stop, :]) - change

            ahead = update(end, end + BLOCK)
            if end + BLOCK < width:
                table[end + BLOCK :, :] = update(end + BLOCK, width)

def basis_kernel(gram, y, r_out, q_out, table):
    unpack_gram(gram, table)
    factor(table, r_out)
    q_out[...] = lax.dot_general(
        y[...],
        table[...],
        (((1,), (1,)), ((), ())),
        precision=HIGH,
        preferred_element_type=jnp.float32,
    )


def orthonormalize(gram, y):
    width = y.shape[1]
    return pl.pallas_call(
        basis_kernel,
        out_shape=[
            jax.ShapeDtypeStruct((width, width), jnp.float32),
            jax.ShapeDtypeStruct(y.shape, jnp.float32),
        ],
        scratch_shapes=[pltpu.VMEM((width, width), jnp.float32)],
        compiler_params=params(),
        name="orthonormalize",
    )(gram, y)


def swap(array, axis, mask):
    size = math.prod(lax.axis_size(name) for name in (axis if isinstance(axis, tuple) else (axis,)))
    return lax.ppermute(array, axis, [(i, i ^ mask) for i in range(size)])


def both(mine, got, first):
    return jnp.concatenate([jnp.where(first, mine, got), jnp.where(first, got, mine)], axis=0)


def gram_total(gram):
    rows, width = gram.shape
    if lax.axis_size("snp") != 4 or lax.axis_size("samp") != 4:
        return lax.psum(gram, ("samp", "snp"))
    bit = jnp.bitwise_and(lax.axis_index("snp"), 1)
    halves = gram.reshape(2, rows // 2, width)
    mine, other = (lax.dynamic_index_in_dim(halves, b, 0, keepdims=False) for b in (bit, 1 - bit))
    part = mine + swap(other, "snp", 1)
    part = part + swap(part, "snp", 2)
    part = part + swap(part, "samp", 1)
    part = part + swap(part, "samp", 2)
    return both(part, swap(part, "snp", 1), bit == 0)


def per_device(genotypes, basis_cols):
    n_snp, n_samp = lax.axis_size("snp"), lax.axis_size("samp")
    bits = n_snp.bit_length() - 1
    words, snps = genotypes.shape
    width = basis_cols.shape[1]
    samples = words * PLANES * n_samp
    inv_root = float(1.0 / samples**0.5)
    chunk = snps // n_samp
    direct = n_samp in (2, 4) and chunk % LANES == 0

    other, sums = project(genotypes, basis_cols, True)
    got = swap(other, "snp", 1)
    more = swap(sums, "snp", 1 << (bits - 1))
    (mine,) = project(genotypes, basis_cols, False)
    *parts, sums = merge(mine, got, sums, more, 2)
    for b in range(bits - 1):
        sums = sums + swap(sums, "snp", 1 << b)
    if n_samp <= 4:
        for b in range(n_samp.bit_length() - 1):
            sums = sums + swap(sums, "samp", 1 << b)
    else:
        sums = lax.psum(sums, "samp")

    kept, received = [], []
    got, sent = None, None
    for group, part in enumerate(parts):
        if got is not None:
            part, _, _ = lax.optimization_barrier((part, got, sums))
        for b in range(1, bits - 1):
            part = part + swap(part, "snp", 1 << b)
        got = swap(part, "snp", 1 << (bits - 1))
        ready = got
        if sent is not None:
            ready, _ = lax.optimization_barrier((got, sent))
        rows = finish(part, ready, sums, samples, group)
        scores = (rows, swap(rows, "snp", 1))
        if direct:
            masks = ((2, 3, 1) if group else (3, 2, 1)) if n_samp == 4 else (1,)
            coded = list(chunks_of_y(genotypes, scores, chunk, inv_root, masks[:1]))
            *others, own = chunks_of_y(genotypes, scores, chunk, inv_root, masks[1:] + (0,))
            coded += others
            kept.append(own)
            received.append([swap(c, "samp", mask) for c, mask in zip(coded, masks)])
            sent = (received[-1][0], own)
        else:
            tile = 4 * LANES if snps % (4 * LANES) == 0 else snps
            tiles = [
                chunks_of_y(genotypes, scores, tile, inv_root, piece=i)[0]
                for i in range(snps // tile)
            ]
            whole = jnp.concatenate(tiles, axis=0)
            kept.append(lax.psum_scatter(whole, "samp", scatter_dimension=0, tiled=True))
            received.append([])
    done = add_chunks(kept[0], received[0]) if direct else kept[0]
    y_local, y_again, gram = collect(done, kept[1], received[1], 1.0 / (snps * n_snp))
    gram_sum = gram_total(gram)
    r_factor, q_next = orthonormalize(gram_sum, y_again)
    layout = (1, 1, y_local.shape[0], width)
    return (y_local.reshape(layout), r_factor, q_next.reshape(layout))


def solution(mesh):
    return jax.shard_map(
        per_device,
        mesh=mesh,
        in_specs=(P(("grp", "samp"), "snp"), P(("grp", "snp"), None)),
        out_specs=(
            P(("grp", "snp"), "samp", None, None),
            P("grp", None),
            P(("grp", "snp"), "samp", None, None),
        ),
        check_vma=False,
    )
```
